128 devices in a mesh: dp: 16 (over x, y), vocab: 8 (over z, core).
Axes of the slice: x: 4, y: 4, z: 4, core: 2. Of those that a mesh axis runs over, the one named last changes fastest.
Arguments:
- pol_hidden: bfloat16 [512, 8192], P(None, 'dp'), may hold values from -82 to 82
- pol_weight: bfloat16 [8192, 65536], P('dp', 'vocab'), may hold values from -0.0625 to 0.0625
- ref_logits: bfloat16 [256, 65536], P('dp', 'vocab'), may hold values from -205 to 205
- targets: int32 [256], replicated, may hold values from 0 to 65535
- owners: int32 [256, 1], replicated, may hold values from 0 to 15; in each aligned block of 16 rows (0 to 15, 16 to 31, ...) at most 2 rows name the same one
- grad_logprob: float32 [512], replicated, may hold values from -9 to 9
- grad_kl: float32 [512], replicated, may hold values from -96 to 96
Outputs:
- token_logprob: float32 [512], P('dp')
- token_kl: float32 [512], P('dp')
- normalizer: float32 [512], P('dp')
- feature_grad: bfloat16 [512, 8192], P('vocab', 'dp')
- weight_grad: bfloat16 [8192, 65536], P('dp', 'vocab')
The draws below stay inside these ranges and needn't reach their ends.
Inputs may be any that keep to these rules, and one draw needn't show every extreme that they name: `owners`: in each aligned block of 16 rows (the rows of one device along dp) no owner is named more than 2 times, a bound that some block reaches.
All inputs are finite; a program needn't handle non-finite values.
Results may differ from the reference program's by a relative error of at most 0.015.
Values may be sent and summed in bfloat16 or wider, within the bound.
A program may use at most 128 MiB of HBM per device.

```python
import math
import jax
import jax.numpy as jnp
import numpy as np

D = 8192
ROWS_DEV = 16
CAPACITY = 2
SLOTS = 32
ALL_SLOTS = 512
TOKENS = 256
VOCAB = 65536
N_DP = 16


def draw_pol_hidden(key, part):
    key = jax.random.fold_in(key, 11)
    key_values = jax.random.fold_in(key, 0)
    values = jax.random.truncated_normal(key_values, -6.0, 6.0, (ALL_SLOTS, D), jnp.float32)
    return values.astype(jnp.bfloat16)


def draw_ref_logits(key, part):
    key = jax.random.fold_in(key, 23)
    key_values = jax.random.fold_in(key, 0)
    values = 2.0 * jax.random.truncated_normal(key_values, -6.0, 6.0, (TOKENS, VOCAB), jnp.float32)
    return values.astype(jnp.bfloat16)


def plant(values, key, smallest, largest):
    longest = values.shape.index(max(values.shape))
    spots = []
    for shift in (0, 1):
        where = [jax.random.randint(jax.random.fold_in(key, axis), (), 0, length) for axis, length in enumerate(values.shape)]
        where[longest] = (where[longest] + shift) % values.shape[longest]
        spots.append(tuple(where))
    return values.at[spots[0]].set(smallest).at[spots[1]].set(largest)


def block_scale(rng, dims, pieces, smallest, high):
    loudness, own = 1.0, jax.random.fold_in(rng, 6)
    for dim, parts in pieces:
        draws = jnp.exp(jax.random.uniform(jax.random.fold_in(own, dim), (parts,), jnp.float32, smallest / len(pieces), high / len(pieces)))
        loudness = loudness * jnp.repeat(draws, dims[dim] // parts).reshape([-1 if axis == dim else 1 for axis in range(len(dims))])
    return loudness


def shared_out(key, own, number, rows, number_of, top, most, skew):
    sequence = jax.random.permutation(key, number_of)
    heavy_load, ordinary = portions_of(number_of, rows * top, most, skew, True), portions_of(number_of, rows * top, most, skew, False)
    places = jnp.arange(number_of)

    def named(sizes, offset_by):
        used = int((sizes > 0).sum())
        fixed = max(1, used // 4)
        passed = fixed + (places - fixed + offset_by * (used - fixed)) % max(1, number_of - fixed)
        return jnp.zeros((number_of,), jnp.int32).at[sequence[jnp.where(places < fixed, places, passed)]].set(jnp.asarray(sizes, jnp.int32))

    sizes = jnp.where(number % 4 == 0, named(heavy_load, number // 4), named(ordinary, number - number // 4 - 1))
    mixed = jax.random.permutation(jax.random.fold_in(own, 3), number_of)
    donor, receiver = mixed[0:number_of // 2 * 2:2], mixed[1:number_of // 2 * 2:2]
    margin = jnp.minimum(sizes[donor] - 1, most - sizes[receiver]) // 2
    margin = jnp.where((donor == sequence[0]) | (receiver == sequence[0]) | (sizes[receiver] == 0), 0, jnp.maximum(margin, 0))
    passed = jax.random.randint(jax.random.fold_in(own, 4), (number_of // 2,), 0, 1 << 20) % (margin + 1)
    sizes = sizes.at[donor].add(-passed).at[receiver].add(passed)
    members = jnp.searchsorted(jnp.cumsum(sizes), jnp.arange(rows * top), side="right").astype(jnp.int32)
    table = members.reshape(top, rows).T
    table = table[jax.random.permutation(jax.random.fold_in(own, 1), rows)]
    offset_by = jax.random.randint(jax.random.fold_in(own, 2), (rows, 1), 0, top)
    return jnp.take_along_axis(table, (jnp.arange(top)[None, :] + offset_by) % top, axis=1)


def portions_of(count, total, limit, slope, full):
    portions = [(1 << 20) // math.isqrt(rank ** slope) + 1 for rank in range(1, count + 1)]
    largest = limit if full else min(limit, max(-(-total // count), total * portions[0] // sum(portions)))
    least = 1 if total - largest >= count - 1 else 0
    given, rest = [largest] + [least] * (count - 1), total - largest - least * (count - 1)
    while rest > 0:
        free = [i for i in range(1, count) if given[i] < largest] or [i for i in range(1, count) if given[i] < limit]
        whole, remaining = sum([portions[i] for i in free]), rest
        for i in free:
            addition = min(limit - given[i], max(1, remaining * portions[i] // whole), rest)
            given[i] = given[i] + addition
            rest = rest - addition
    return np.array(given)


def normal_values(own_key, extent, width, bound, cuts=(), kind=jnp.bfloat16):
    values = width * jax.random.normal(own_key, extent, jnp.float32)
    if cuts:
        values = values * block_scale(own_key, extent, cuts, -0.22, 0.18)
    return jnp.clip(values, -bound, bound).astype(kind)


def setup_inputs(seed: int = 0) -> dict:
    streams_of = jax.random.split(jax.random.key(seed), 8)
    pol_hidden = draw_pol_hidden(jax.random.fold_in(streams_of[7], 71), 0)
    pol_weight = normal_values(streams_of[1], (D, VOCAB), D ** -0.5, 0.0625, ((0, 16), (1, 8)))
    ref_logits = draw_ref_logits(jax.random.fold_in(streams_of[7], 71), 0)
    targets = plant(jax.random.randint(streams_of[3], (TOKENS,), 0, VOCAB), jax.random.fold_in(streams_of[3], 1), 0, VOCAB - 1).astype(jnp.int32)
    owners_keys = jax.random.split(jax.random.fold_in(streams_of[4], 1), TOKENS // ROWS_DEV)
    owners_turns = jax.random.permutation(jax.random.fold_in(streams_of[4], 3), TOKENS // ROWS_DEV)
    owners = jax.vmap(lambda own, number: shared_out(jax.random.fold_in(streams_of[4], 2), own, number, ROWS_DEV, N_DP, 1, CAPACITY, 2))(owners_keys, owners_turns).reshape((TOKENS, 1))
    grad_logprob = normal_values(streams_of[5], (ALL_SLOTS,), 1.5, 9.0, (), jnp.float32)
    grad_kl = normal_values(streams_of[6], (ALL_SLOTS,), 16.0, 96.0, (), jnp.float32)
    return {"pol_hidden": pol_hidden, "pol_weight": pol_weight, "ref_logits": ref_logits, "targets": targets, "owners": owners, "grad_logprob": grad_logprob, "grad_kl": grad_kl}


def slot_numbers(owners):
    target_owner = owners[:, 0].astype(jnp.int32)
    columns = jnp.arange(N_DP, dtype=jnp.int32)
    onehot = (target_owner[:, None] == columns[None, :]).astype(jnp.int32)
    blocks = onehot.reshape(N_DP, ROWS_DEV, N_DP)
    before = jnp.sum((jnp.cumsum(blocks, axis=1) - blocks) * blocks, axis=2).reshape(TOKENS)
    source = jnp.arange(TOKENS, dtype=jnp.int32) // ROWS_DEV
    return (target_owner * SLOTS + source * CAPACITY + before).astype(jnp.int32)


def reference(pol_hidden, pol_weight, ref_logits, targets, owners, grad_logprob, grad_kl):
    slot_of = slot_numbers(owners)
    row_hidden = pol_hidden[slot_of]
    logits = jnp.dot(row_hidden, pol_weight, preferred_element_type=jnp.float32)
    row_norm = jax.nn.logsumexp(logits, axis=1)
    ref_values = ref_logits.astype(jnp.float32)
    ref_norm = jax.nn.logsumexp(ref_values, axis=1)
    probs = jnp.exp(logits - row_norm[:, None])
    excess = logits - row_norm[:, None] - ref_values + ref_norm[:, None]
    row_kl = jnp.sum(probs * excess, axis=1)
    is_target = jnp.arange(VOCAB, dtype=jnp.int32)[None, :] == targets.astype(jnp.int32)[:, None]
    row_logprob = jnp.sum(jnp.where(is_target, logits, 0.0), axis=1) - row_norm
    lp_cotangent = grad_logprob[slot_of]
    kl_cotangent = grad_kl[slot_of]
    logit_grads = (lp_cotangent[:, None] * is_target.astype(jnp.float32)
                   + probs * (kl_cotangent[:, None] * (excess - row_kl[:, None]) - lp_cotangent[:, None])).astype(jnp.bfloat16)
    feature = jnp.dot(logit_grads, pol_weight.T, preferred_element_type=jnp.float32).astype(jnp.bfloat16)
    weight_grad = jnp.dot(row_hidden.T, logit_grads, preferred_element_type=jnp.float32).astype(jnp.bfloat16)
    feature_grad = jnp.zeros((ALL_SLOTS, D), jnp.bfloat16).at[slot_of].set(feature)
    token_logprob = jnp.zeros((ALL_SLOTS,), jnp.float32).at[slot_of].set(row_logprob)
    token_kl = jnp.zeros((ALL_SLOTS,), jnp.float32).at[slot_of].set(row_kl)
    normalizer = jnp.zeros((ALL_SLOTS,), jnp.float32).at[slot_of].set(row_norm)
    return (token_logprob, token_kl, normalizer, feature_grad, weight_grad)
```

```python
import jax
import jax.numpy as jnp
from jax import lax
from jax.sharding import PartitionSpec as P


def routing(owners, dp_count, rows_dev, capacity):
    target_owner = owners[:, 0]
    total_rows = target_owner.shape[0]
    columns = lax.broadcasted_iota(jnp.int32, (total_rows, dp_count), 1)
    onehot = (target_owner[:, None] == columns).astype(jnp.int32)
    blocks = onehot.reshape(dp_count, rows_dev, dp_count)
    before = jnp.sum((jnp.cumsum(blocks, axis=1) - blocks) * blocks, axis=2).reshape(total_rows)
    source = lax.broadcasted_iota(jnp.int32, (total_rows,), 0) // rows_dev
    slot_of = target_owner * (dp_count * capacity) + source * capacity + before
    return (slot_of, target_owner * capacity + before)


def local_stats(logits, ref_values, target, first_col):
    row_peak = jnp.max(logits, axis=1)
    weights = jnp.exp(logits - row_peak[:, None])
    row_mass = jnp.sum(weights, axis=1)
    row_cross = jnp.sum(weights * (logits - ref_values), axis=1)
    ref_peak = jnp.max(ref_values, axis=1)
    ref_mass = jnp.sum(jnp.exp(ref_values - ref_peak[:, None]), axis=1)
    vocab_ids = first_col + lax.broadcasted_iota(jnp.int32, logits.shape, 1)
    picked = jnp.sum(jnp.where(vocab_ids == target[:, None], logits, 0.0), axis=1)
    return (row_peak, row_mass, row_cross, ref_peak, ref_mass, picked)


def combine(earlier, later):
    joint_peak = jnp.maximum(earlier[0], later[0])
    left_scale = jnp.exp(earlier[0] - joint_peak)
    right_scale = jnp.exp(later[0] - joint_peak)
    joint_ref = jnp.maximum(earlier[3], later[3])
    ref_mass = earlier[4] * jnp.exp(earlier[3] - joint_ref) + later[4] * jnp.exp(
        later[3] - joint_ref
    )
    return (
        joint_peak,
        earlier[1] * left_scale + later[1] * right_scale,
        earlier[2] * left_scale + later[2] * right_scale,
        joint_ref,
        ref_mass,
        earlier[5] + later[5],
    )


def finish(totals):
    row_peak, row_mass, row_cross, ref_peak, ref_mass, picked = totals
    log_norm = row_peak + jnp.log(row_mass)
    ref_norm = ref_peak + jnp.log(ref_mass)
    row_kl = row_cross / row_mass - log_norm + ref_norm
    return (log_norm, ref_norm, row_kl, picked - log_norm)


def logit_grad(
    logits,
    ref_values,
    target,
    first_col,
    log_norm,
    ref_norm,
    row_kl,
    lp_cotangent,
    kl_cotangent,
    filled,
):
    probs = jnp.exp(logits - log_norm[:, None])
    vocab_ids = first_col + lax.broadcasted_iota(jnp.int32, logits.shape, 1)
    is_target = (vocab_ids == target[:, None]).astype(jnp.float32)
    excess = logits - log_norm[:, None] - ref_values + ref_norm[:, None] - row_kl[:, None]
    result = lp_cotangent[:, None] * is_target + probs * (
        kl_cotangent[:, None] * excess - lp_cotangent[:, None]
    )
    return (result * filled[:, None]).astype(jnp.bfloat16)


def per_device(pol_hidden, pol_weight, ref_logits, targets, owners, grad_logprob, grad_kl):
    dp_count = lax.axis_size("dp")
    dp_index = lax.axis_index("dp")
    vocab_index = lax.axis_index("vocab")
    rows_dev = ref_logits.shape[0]
    vocab_dev = ref_logits.shape[1]
    all_slots = pol_hidden.shape[0]
    slot_count = all_slots // dp_count
    capacity = slot_count // dp_count
    first_col = vocab_index * vocab_dev
    slot_of, _ = routing(owners, dp_count, rows_dev, capacity)
    placing = slot_of[:, None] == lax.broadcasted_iota(
        jnp.int32, (slot_of.shape[0], all_slots), 1
    )
    row_hidden = jnp.dot(
        placing.astype(jnp.bfloat16), pol_hidden, preferred_element_type=jnp.float32
    ).astype(jnp.bfloat16)
    logits = lax.psum_scatter(
        jnp.dot(row_hidden, pol_weight, preferred_element_type=jnp.float32),
        "dp",
        scatter_dimension=0,
        tiled=True,
    )
    own = lax.dynamic_slice_in_dim(placing, dp_index * rows_dev, rows_dev)
    lp_cotangent = jnp.sum(jnp.where(own, grad_logprob[None, :], 0.0), axis=1)
    kl_cotangent = jnp.sum(jnp.where(own, grad_kl[None, :], 0.0), axis=1)
    target = lax.dynamic_slice_in_dim(targets, dp_index * rows_dev, rows_dev)
    ref_values = ref_logits.astype(jnp.float32)
    stats = jnp.stack(local_stats(logits, ref_values, target, first_col))
    stats = lax.all_gather(stats, "vocab")
    totals = tuple(stats[0])
    for part in range(1, stats.shape[0]):
        totals = combine(totals, tuple(stats[part]))
    log_norm, ref_norm, row_kl, row_logprob = finish(totals)
    logit_grads = logit_grad(
        logits,
        ref_values,
        target,
        first_col,
        log_norm,
        ref_norm,
        row_kl,
        lp_cotangent,
        kl_cotangent,
        jnp.ones_like(log_norm),
    )
    gathered = lax.all_gather(logit_grads, "dp", axis=0, tiled=True)
    rows = lax.all_gather(jnp.stack([row_logprob, row_kl, log_norm]), "dp", axis=1, tiled=True)
    mine = lax.dynamic_slice_in_dim(placing, dp_index * slot_count, slot_count, axis=1)
    results = jnp.sum(jnp.where(mine[None], rows[:, :, None], 0.0), axis=1)
    feature_rows = lax.dot_general(
        gathered, pol_weight, (((1,), (1,)), ((), ())), preferred_element_type=jnp.float32
    )
    feature_terms = lax.dot_general(
        placing.astype(jnp.float32),
        feature_rows,
        (((0,), (0,)), ((), ())),
        precision=lax.Precision.HIGHEST,
        preferred_element_type=jnp.float32,
    )
    weight_grad = lax.dot_general(
        row_hidden, gathered, (((0,), (0,)), ((), ())), preferred_element_type=jnp.float32
    ).astype(jnp.bfloat16)
    feature_grad = lax.psum_scatter(feature_terms, "vocab", scatter_dimension=0, tiled=True).astype(
        jnp.bfloat16
    )
    return (results[0], results[1], results[2], feature_grad, weight_grad)


def solution(mesh):
    in_specs = (P(None, "dp"), P("dp", "vocab"), P("dp", "vocab"), P(), P(), P(), P())
    out_specs = (P("dp"), P("dp"), P("dp"), P("vocab", "dp"), P("dp", "vocab"))
    return jax.shard_map(
        per_device, mesh=mesh, in_specs=in_specs, out_specs=out_specs, check_vma=False
    )
```

```python
import functools

import jax
import jax.numpy as jnp
from jax import lax
from jax.experimental import pallas as pl
from jax.experimental.pallas import tpu as pltpu
from jax.sharding import PartitionSpec as P

F32 = jnp.float32
BF16 = jnp.bfloat16
I32 = jnp.int32
MESH = pl.DeviceIdType.MESH
SIDE = 4
LANES = 128
SUBS = 4
WIDE = 2
FLOWS = ((0, 1), (0, -1), (1, 1), (1, -1))
LARGEST = 32766.0


def encode(blocks, dst):
    width = blocks[0].shape[1]
    tiles = width // LANES
    parts = []
    for block in blocks:
        for t in range(tiles):
            cols = slice(t * LANES, (t + 1) * LANES)
            parts.append((block[0:8, cols], block[8:16, cols]))
    peak = jnp.full((8, LANES), 1e-30, F32)
    for high, low in parts:
        peak = jnp.maximum(peak, jnp.maximum(jnp.abs(high), jnp.abs(low)))
    power = jnp.ceil(jnp.log2(peak) * 8.0)
    inverse = jnp.exp2(power * -0.125) * LARGEST
    for k, (high, low) in enumerate(parts):
        high_code = jnp.round(high * inverse).astype(I32)
        low_code = jnp.round(low * inverse).astype(I32)
        dst[:, k * LANES : (k + 1) * LANES] = (high_code << 16) | (low_code & 0xFFFF)
    end = len(parts) * LANES
    dst[:, end : end + LANES] = power.astype(I32)


def decode(src, block, width):
    end = src.shape[1] - LANES
    scale = jnp.exp2(src[:, end : end + LANES].astype(F32) * 0.125) * (1.0 / LARGEST)
    highs, lows = [], []
    for t in range(width // LANES):
        start = block * width + t * LANES
        word = src[:, start : start + LANES]
        highs.append((word >> 16).astype(F32) * scale)
        lows.append(((word << 16) >> 16).astype(F32) * scale)
    return jnp.concatenate(
        [jnp.concatenate(highs, axis=1), jnp.concatenate(lows, axis=1)], axis=0
    )


def head_kernel(
    vocab_count,
    hidden,
    weight_hbm,
    ref,
    target,
    owner_col,
    owner_row,
    cot_lp,
    cot_kl,
    grads_out,
    rows_out,
    feature_out,
    tokens_out,
    weight,
    part,
    send1,
    recv1,
    send2,
    recv2,
    logits,
    grads,
    peaks,
    cots,
    stats,
    tokens,
    feature,
    slots,
    core_recv,
    zsend,
    zrecv,
    w_sem,
    rs_send,
    rs_recv,
    ag_send,
    ag_recv,
    st_send,
    st_recv,
    tk_send,
    tk_recv,
    core_send_sem,
    core_recv_sem,
    z_send,
    z_recv,
    out_sem,
):
    subs, _, _, width = weight.shape
    pieces = grads.shape[0]
    rows_all = hidden.shape[0]
    count = owner_col.shape[0]
    chips = SIDE * SIDE
    rows_dev = count // chips
    levels = vocab_count // 2
    flow_width = subs * width
    dp = lax.axis_index("dp")
    vocab = lax.axis_index("vocab")
    here = (dp // SIDE, dp % SIDE)
    level, core = vocab // 2, vocab % 2

    barrier = pltpu.get_barrier_semaphore()
    for step in range(1, chips):
        pl.semaphore_signal(
            barrier, inc=1, device_id=((dp + step) % chips, vocab), device_id_type=MESH
        )
    for step in range(1, vocab_count):
        pl.semaphore_signal(
            barrier, inc=1, device_id=(dp, (vocab + step) % vocab_count), device_id_type=MESH
        )

    def weight_copy(s, f):
        cols = pl.ds(pl.multiple_of(f * flow_width + s * width, LANES), width)
        return pltpu.make_async_copy(weight_hbm.at[:, cols], weight.at[s, f], w_sem.at[s, f])

    for s in range(subs):
        for f in range(4):
            weight_copy(s, f).start()

    def iota(shape, dim):
        return lax.broadcasted_iota(I32, shape, dim)

    rows_i, cols_i = iota((count, count), 0), iota((count, count), 1)
    alike = (owner_col[...] == owner_row[...]) & (rows_i // rows_dev == cols_i // rows_dev)
    before_col = jnp.sum(jnp.where(alike & (cols_i < rows_i), 1.0, 0.0), axis=1, keepdims=True)
    before_row = jnp.sum(jnp.where(alike & (rows_i < cols_i), 1.0, 0.0), axis=0, keepdims=True)
    slot_count = rows_all // chips
    capacity = slot_count // chips
    slot_col = (
        owner_col[...] * slot_count
        + (iota((count, 1), 0) // rows_dev) * capacity
        + before_col.astype(I32)
    )
    slot_row = (
        owner_row[...] * slot_count
        + (iota((1, count), 1) // rows_dev) * capacity
        + before_row.astype(I32)
    )
    placing = slot_col == iota((count, rows_all), 1)
    rows_out[...] = jnp.dot(
        jnp.where(placing, 1.0, 0.0).astype(BF16), hidden[...], preferred_element_type=F32
    ).astype(BF16)
    lp_col = jnp.sum(jnp.where(placing, cot_lp[...], 0.0), axis=1, keepdims=True)
    kl_col = jnp.sum(jnp.where(placing, cot_kl[...], 0.0), axis=1, keepdims=True)
    lane_all = iota((count, LANES), 1)
    cots[...] = jnp.where(lane_all == 0, lp_col, 0.0) + jnp.where(lane_all == 1, kl_col, 0.0)

    def along(axis, offset):
        return lax.rem(here[axis] + offset + SIDE, SIDE)

    def device(axis, offset):
        moved = along(axis, offset)
        return (moved * SIDE + here[1], vocab) if axis == 0 else (here[0] * SIDE + moved, vocab)

    def place(f, first, second):
        return (first, second) if FLOWS[f][0] == 0 else (second, first)

    def rs_copy(s, f, kind):
        axis, way = FLOWS[f]
        stage, role = kind // 3, kind % 3
        if stage == 1:
            axis = 1 - axis
        source, landing = (send1, recv1) if stage == 0 else (send2, recv2)
        return pltpu.make_async_remote_copy(
            src_ref=source.at[s, f, role],
            dst_ref=landing.at[s, f, role],
            send_sem=rs_send.at[s, f, kind],
            recv_sem=rs_recv.at[s, f, kind],
            device_id=device(axis, -way if role == 1 else way),
            device_id_type=MESH,
        )

    def first_blocks(s, f, offset):
        first = along(FLOWS[f][0], offset)
        return [part[(s, f) + place(f, first, k)] for k in range(SIDE)]

    def second_block(s, f, offset):
        axis = FLOWS[f][0]
        return part[(s, f) + place(f, here[axis], along(1 - axis, offset))]

    def multiply(s):
        for f in range(4):
            weight_copy(s, f).wait()
            product = jnp.dot(rows_out[...], weight[s, f], preferred_element_type=F32)
            part[s, f] = product.reshape(SIDE, SIDE, rows_dev, width)

    def first_send(s):
        for f in range(4):
            way = FLOWS[f][1]
            encode(first_blocks(s, f, 2), send1.at[s, f, 0])
            encode(first_blocks(s, f, -way), send1.at[s, f, 1])
        for f in range(4):
            rs_copy(s, f, 0).start()
            rs_copy(s, f, 1).start()

    def first_relay(s):
        for f in range(4):
            rs_copy(s, f, 0).wait_recv()
        for f in range(4):
            own = first_blocks(s, f, FLOWS[f][1])
            arrived = recv1.at[s, f, 0]
            encode(
                [own[k] + decode(arrived, k, width) for k in range(SIDE)], send1.at[s, f, 2]
            )
        for f in range(4):
            rs_copy(s, f, 2).start()

    def first_sum(s):
        for f in range(4):
            rs_copy(s, f, 1).wait_recv()
            rs_copy(s, f, 2).wait_recv()
        for f in range(4):
            axis, way = FLOWS[f]
            for k in range(SIDE):
                spot = (s, f) + place(f, here[axis], k)
                part[spot] = (
                    part[spot]
                    + decode(recv1.at[s, f, 1], k, width)
                    + decode(recv1.at[s, f, 2], k, width)
                )
        for f in range(4):
            way = FLOWS[f][1]
            encode([second_block(s, f, 2)], send2.at[s, f, 0])
            encode([second_block(s, f, -way)], send2.at[s, f, 1])
        for f in range(4):
            rs_copy(s, f, 3).start()
            rs_copy(s, f, 4).start()

    def second_relay(s):
        for f in range(4):
            rs_copy(s, f, 3).wait_recv()
        for f in range(4):
            encode(
                [second_block(s, f, FLOWS[f][1]) + decode(recv2.at[s, f, 0], 0, width)],
                send2.at[s, f, 2],
            )
        for f in range(4):
            rs_copy(s, f, 5).start()

    def second_sum(s):
        for f in range(4):
            rs_copy(s, f, 4).wait_recv()
            rs_copy(s, f, 5).wait_recv()
        peak = peaks[...]
        for f in range(4):
            done = (
                second_block(s, f, 0)
                + decode(recv2.at[s, f, 1], 0, width)
                + decode(recv2.at[s, f, 2], 0, width)
            )
            logits[s, f] = done
            for t in range(width // LANES):
                peak = jnp.maximum(peak, done[:, t * LANES : (t + 1) * LANES])
        peaks[...] = peak

    def ref_piece(s, f):
        cols = pl.ds(pl.multiple_of(f * flow_width + s * width, LANES), width)
        return ref[:, cols].astype(F32)

    def lane_sum(values):
        total = values[:, 0:LANES]
        for t in range(1, width // LANES):
            total = total + values[:, t * LANES : (t + 1) * LANES]
        return total

    peaks[...] = jnp.full((rows_dev, LANES), -jnp.inf, F32)
    multiply(0)
    pl.semaphore_wait(barrier, chips - 1 + vocab_count - 1)
    first_send(0)

    def ref_max(s, so_far):
        for f in range(4):
            so_far = jnp.maximum(so_far, jnp.max(ref_piece(s, f), axis=1, keepdims=True))
        return so_far

    ref_peak = lax.fori_loop(0, subs, ref_max, jnp.full((rows_dev, 1), -jnp.inf, F32))

    def ref_sum(s, so_far):
        for f in range(4):
            so_far = so_far + lane_sum(jnp.exp(ref_piece(s, f) - ref_peak))
        return so_far

    ref_mass = jnp.sum(
        lax.fori_loop(0, subs, ref_sum, jnp.zeros((rows_dev, LANES), F32)), axis=1, keepdims=True
    )

    def rs_step(step, carry):
        @pl.when(step < subs)
        def _():
            multiply(step)
            first_send(step)

        @pl.when(step - 1 < subs)
        def _():
            first_relay(step - 1)

        @pl.when((step >= 2) & (step - 2 < subs))
        def _():
            first_sum(step - 2)

        @pl.when((step >= 3) & (step - 3 < subs))
        def _():
            second_relay(step - 3)

        @pl.when(step >= 4)
        def _():
            second_sum(step - 4)

        return carry

    lax.fori_loop(1, subs + 4, rs_step, 0)

    peak = jnp.max(peaks[...], axis=1, keepdims=True)
    mine = pl.ds(pl.multiple_of(dp * rows_dev, rows_dev), rows_dev)
    my_target = target[mine, :]
    first_col = vocab * (4 * flow_width)

    def hit(s, f):
        ids = first_col + f * flow_width + s * width + iota((rows_dev, width), 1)
        return ids == my_target

    def sums(s, so_far):
        mass, cross, picked = so_far
        for f in range(4):
            values = logits[s, f]
            weights = jnp.exp(values - peak)
            mass = mass + lane_sum(weights)
            cross = cross + lane_sum(weights * (values - ref_piece(s, f)))
            picked = picked + lane_sum(jnp.where(hit(s, f), values, 0.0))
        return mass, cross, picked

    nothing = jnp.zeros((rows_dev, LANES), F32)
    mass, cross, picked = [
        jnp.sum(value, axis=1, keepdims=True)
        for value in lax.fori_loop(0, subs, sums, (nothing, nothing, nothing))
    ]
    lane = iota((rows_dev, LANES), 1)
    packed = nothing
    for k, value in enumerate((peak, mass, cross, ref_peak, ref_mass, picked)):
        packed = packed + jnp.where(lane == k, value, 0.0)
    stats[vocab] = packed

    def stats_copy(step):
        return pltpu.make_async_remote_copy(
            src_ref=stats.at[vocab],
            dst_ref=stats.at[vocab],
            send_sem=st_send.at[step],
            recv_sem=st_recv.at[step],
            device_id=(dp, (vocab + step) % vocab_count),
            device_id_type=MESH,
        )

    for step in range(1, vocab_count):
        stats_copy(step).start()
    for step in range(1, vocab_count):
        stats_copy(step).wait_recv()
    every = [stats[k] for k in range(vocab_count)]
    peak, ref_peak = every[0][:, 0:1], every[0][:, 3:4]
    for tile in every[1:]:
        peak = jnp.maximum(peak, tile[:, 0:1])
        ref_peak = jnp.maximum(ref_peak, tile[:, 3:4])
    mass, cross, ref_mass, picked = 0.0, 0.0, 0.0, 0.0
    for tile in every:
        scale = jnp.exp(tile[:, 0:1] - peak)
        mass = mass + tile[:, 1:2] * scale
        cross = cross + tile[:, 2:3] * scale
        ref_mass = ref_mass + tile[:, 4:5] * jnp.exp(tile[:, 3:4] - ref_peak)
        picked = picked + tile[:, 5:6]
    norm = peak + jnp.log(mass)
    ref_norm = ref_peak + jnp.log(ref_mass)
    row_kl = cross / mass - norm + ref_norm
    tokens[dp] = (
        jnp.where(lane == 0, picked - norm, 0.0)
        + jnp.where(lane == 1, row_kl, 0.0)
        + jnp.where(lane == 2, norm, 0.0)
    )

    my_cots = cots[mine, :]
    lp, kl = my_cots[:, 0:1], my_cots[:, 1:2]
    shift = ref_norm - norm - row_kl
    wide = subs // pieces

    def gradients(g):
        for f in range(4):
            for w in range(wide):
                s = g * wide + w
                values = logits[s, f]
                probs = jnp.exp(values - norm)
                excess = values - ref_piece(s, f) + shift
                result = jnp.where(hit(s, f), lp, 0.0) + probs * (kl * excess - lp)
                grads[g, f, here[0], here[1], :, w * width : (w + 1) * width] = result.astype(BF16)

    def ag_copy(g, f, kind):
        axis, way = FLOWS[f]
        other = 1 - axis
        if kind < 3:
            spot = place(f, along(axis, -way if kind == 2 else 0), here[other])
            to = device(axis, -way if kind == 1 else way)
        else:
            k, role = (kind - 3) // 3, (kind - 3) % 3
            first = along(axis, (0, -way, way, 2)[k])
            spot = place(f, first, along(other, -way if role == 2 else 0))
            to = device(other, -way if role == 1 else way)
        block = grads.at[(g, f) + spot]
        return pltpu.make_async_remote_copy(
            src_ref=block,
            dst_ref=block,
            send_sem=ag_send.at[g, f, kind],
            recv_sem=ag_recv.at[g, f, kind],
            device_id=to,
            device_id_type=MESH,
        )

    def ag_start(g):
        gradients(g)
        for kind in (0, 1, 3, 4):
            for f in range(4):
                ag_copy(g, f, kind).start()

    def ag_pass(g, steps):
        for wait, starts in steps:
            for f in range(4):
                ag_copy(g, f, wait).wait_recv()
                for kind in starts:
                    ag_copy(g, f, kind).start()

    def ag_relay(g):
        ag_pass(g, ((0, (2, 6, 7)), (1, (9, 10)), (3, (5,)), (2, (12, 13))))

    def ag_finish(g):
        ag_pass(g, ((6, (8,)), (9, (11,)), (12, (14,))))
        ag_pass(g, tuple((kind, ()) for kind in (4, 7, 10, 13, 5, 8, 11, 14)))

    def out_copy(g, f):
        cols = pl.ds(pl.multiple_of(f * flow_width + g * wide * width, LANES), wide * width)
        return pltpu.make_async_copy(
            grads.at[g, f], grads_out.at[:, :, :, cols], out_sem.at[g, f]
        )

    def feature_step(g):
        for f in range(4):
            out_copy(g, f).start()
        total = feature[...]
        for f in range(4):
            for w in range(wide):
                rows = grads[g, f, :, :, :, w * width : (w + 1) * width].reshape(count, width)
                total = total + lax.dot_general(
                    rows,
                    weight[g * wide + w, f],
                    (((1,), (1,)), ((), ())),
                    preferred_element_type=F32,
                )
        feature[...] = total

    def tokens_copy(step):
        return pltpu.make_async_remote_copy(
            src_ref=tokens.at[dp],
            dst_ref=tokens.at[dp],
            send_sem=tk_send.at[step],
            recv_sem=tk_recv.at[step],
            device_id=((dp + step) % chips, vocab),
            device_id_type=MESH,
        )

    feature[...] = jnp.zeros_like(feature)

    def start_all(g, carry):
        ag_start(g)
        return carry

    lax.fori_loop(0, pieces, start_all, 0)
    for step in range(1, chips):
        tokens_copy(step).start()

    def relay_all(g, carry):
        ag_relay(g)
        return carry

    lax.fori_loop(0, pieces, relay_all, 0)

    def finish_all(g, carry):
        ag_finish(g)
        feature_step(g)
        return carry

    lax.fori_loop(0, pieces, finish_all, 0)

    total = feature[...]
    spread = jnp.where(iota((rows_all, count), 0) == slot_row, 1.0, 0.0).astype(BF16)
    high = total.astype(BF16)
    rest = total - high.astype(F32)
    middle = rest.astype(BF16)
    low = (rest - middle.astype(F32)).astype(BF16)
    placed = jnp.dot(spread, high, preferred_element_type=F32)
    placed = placed + jnp.dot(spread, middle, preferred_element_type=F32)
    placed = placed + jnp.dot(spread, low, preferred_element_type=F32)
    slots[...] = placed.reshape(slots.shape)
    core_copy = pltpu.make_async_remote_copy(
        src_ref=slots.at[:, 1 - core],
        dst_ref=core_recv,
        send_sem=core_send_sem,
        recv_sem=core_recv_sem,
        device_id=(dp, level * 2 + 1 - core),
        device_id_type=MESH,
    )
    core_copy.start()

    for step in range(1, chips):
        tokens_copy(step).wait_recv()
    everyone = tokens[...].reshape(count, LANES)
    mine_slots = slot_col == dp * slot_count + lane_all
    mine_slots = mine_slots & (lane_all < slot_count)
    for k in range(3):
        tokens_out[k : k + 1, :] = jnp.sum(
            jnp.where(mine_slots, everyone[:, k : k + 1], 0.0), axis=0, keepdims=True
        )

    core_copy.wait_recv()
    slot_rows = slots.shape[2]
    feature_width = slots.shape[3]

    def pair_sum(l):
        return slots[l, core] + core_recv[l]

    def z_copy(step):
        return pltpu.make_async_remote_copy(
            src_ref=zsend.at[step],
            dst_ref=zrecv.at[step],
            send_sem=z_send.at[step],
            recv_sem=z_recv.at[step],
            device_id=(dp, ((level + step) % levels) * 2 + core),
            device_id_type=MESH,
        )

    for step in (2, 1, 3):
        if step < levels:
            both = pair_sum((level + step) % levels)
            encode([both[k : k + 16] for k in range(0, slot_rows, 16)], zsend.at[step])
            z_copy(step).start()
    total = pair_sum(level)
    for step in range(1, levels):
        z_copy(step).wait_recv()
    pieces_out = []
    for k in range(slot_rows // 16):
        block = total[k * 16 : (k + 1) * 16]
        for step in range(1, levels):
            block = block + decode(zrecv.at[step], k, feature_width)
        pieces_out.append(block)
    feature_out[...] = jnp.concatenate(pieces_out, axis=0).astype(BF16)

    def rs_drain(s, carry):
        for f in range(4):
            for kind in range(6):
                rs_copy(s, f, kind).wait_send()
        return carry

    lax.fori_loop(0, subs, rs_drain, 0)

    def ag_drain(g, carry):
        for f in range(4):
            for kind in range(15):
                ag_copy(g, f, kind).wait_send()
            out_copy(g, f).wait()
        return carry

    lax.fori_loop(0, pieces, ag_drain, 0)
    for step in range(1, vocab_count):
        stats_copy(step).wait_send()
    for step in range(1, chips):
        tokens_copy(step).wait_send()
    core_copy.wait_send()
    for step in range(1, levels):
        z_copy(step).wait_send()


def weight_kernel(rows, grads, out):
    block = grads[...].reshape(rows.shape[0], grads.shape[3])
    out[...] = lax.dot_general(
        rows[...], block, (((0,), (0,)), ((), ())), preferred_element_type=F32
    ).astype(BF16)


def per_device(
    vocab_count, pol_hidden, pol_weight, ref_logits, targets, owners, grad_logprob, grad_kl
):
    all_slots, depth = pol_hidden.shape
    cols = pol_weight.shape[1]
    rows_dev = ref_logits.shape[0]
    count = owners.shape[0]
    chips = SIDE * SIDE
    width = cols // (4 * SUBS)
    pieces = SUBS // WIDE
    levels = vocab_count // 2
    slot_rows = all_slots // vocab_count
    unit1 = (SUBS, 4, 3, 8, SIDE * width + LANES)
    unit2 = (SUBS, 4, 3, 8, width + LANES)
    unit3 = (levels, 8, slot_rows // 16 * depth + LANES)
    vmem = pl.BlockSpec(memory_space=pltpu.VMEM)
    anywhere = pl.BlockSpec(memory_space=pl.ANY)
    flops = 2 * count * depth * cols * 2
    grads, rows, feature, tokens = pl.pallas_call(
        functools.partial(head_kernel, vocab_count),
        out_shape=(
            jax.ShapeDtypeStruct((SIDE, SIDE, rows_dev, cols), BF16),
            jax.ShapeDtypeStruct((count, depth), BF16),
            jax.ShapeDtypeStruct((slot_rows, depth), BF16),
            jax.ShapeDtypeStruct((8, LANES), F32),
        ),
        in_specs=[vmem, anywhere] + [vmem] * 6,
        out_specs=(anywhere, vmem, vmem, vmem),
        scratch_shapes=[
            pltpu.VMEM((SUBS, 4, depth, width), BF16),
            pltpu.VMEM((SUBS, 4, SIDE, SIDE, rows_dev, width), F32),
            pltpu.VMEM(unit1, I32),
            pltpu.VMEM(unit1, I32),
            pltpu.VMEM(unit2, I32),
            pltpu.VMEM(unit2, I32),
            pltpu.VMEM((SUBS, 4, rows_dev, width), F32),
            pltpu.VMEM((pieces, 4, SIDE, SIDE, rows_dev, width * WIDE), BF16),
            pltpu.VMEM((rows_dev, LANES), F32),
            pltpu.VMEM((count, LANES), F32),
            pltpu.VMEM((vocab_count, rows_dev, LANES), F32),
            pltpu.VMEM((chips, rows_dev, LANES), F32),
            pltpu.VMEM((count, depth), F32),
            pltpu.VMEM((levels, 2, slot_rows, depth), F32),
            pltpu.VMEM((levels, slot_rows, depth), F32),
            pltpu.VMEM(unit3, I32),
            pltpu.VMEM(unit3, I32),
            pltpu.SemaphoreType.DMA((SUBS, 4)),
            pltpu.SemaphoreType.DMA((SUBS, 4, 6)),
            pltpu.SemaphoreType.DMA((SUBS, 4, 6)),
            pltpu.SemaphoreType.DMA((pieces, 4, 15)),
            pltpu.SemaphoreType.DMA((pieces, 4, 15)),
            pltpu.SemaphoreType.DMA((vocab_count,)),
            pltpu.SemaphoreType.DMA((vocab_count,)),
            pltpu.SemaphoreType.DMA((chips,)),
            pltpu.SemaphoreType.DMA((chips,)),
            pltpu.SemaphoreType.DMA,
            pltpu.SemaphoreType.DMA,
            pltpu.SemaphoreType.DMA((levels,)),
            pltpu.SemaphoreType.DMA((levels,)),
            pltpu.SemaphoreType.DMA((pieces, 4)),
        ],
        compiler_params=pltpu.CompilerParams(
            collective_id=0, has_side_effects=True, vmem_limit_bytes=56 * 2**20
        ),
        cost_estimate=pl.CostEstimate(
            flops=flops, bytes_accessed=3 * depth * cols, transcendentals=3 * rows_dev * cols
        ),
        name="head",
    )(
        pol_hidden,
        pol_weight,
        ref_logits,
        targets.reshape(count, 1),
        owners,
        owners.reshape(1, count),
        grad_logprob.reshape(1, all_slots),
        grad_kl.reshape(1, all_slots),
    )
    tile = min(cols, 1024)
    weight_grad = pl.pallas_call(
        weight_kernel,
        grid=(cols // tile,),
        out_shape=jax.ShapeDtypeStruct((depth, cols), BF16),
        in_specs=[
            pl.BlockSpec((count, depth), lambda i: (0, 0)),
            pl.BlockSpec((SIDE, SIDE, rows_dev, tile), lambda i: (0, 0, 0, i)),
        ],
        out_specs=pl.BlockSpec((depth, tile), lambda i: (0, i)),
        compiler_params=pltpu.CompilerParams(vmem_limit_bytes=32 * 2**20),
        cost_estimate=pl.CostEstimate(
            flops=2 * count * depth * cols, bytes_accessed=2 * (depth + count) * cols, transcendentals=0
        ),
        name="weight_grad",
    )(rows, grads)
    slot_count = all_slots // chips
    return (
        tokens[0, :slot_count],
        tokens[1, :slot_count],
        tokens[2, :slot_count],
        feature,
        weight_grad,
    )


def solution(mesh):
    in_specs = (P(None, "dp"), P("dp", "vocab"), P("dp", "vocab"), P(), P(), P(), P())
    out_specs = (P("dp"), P("dp"), P("dp"), P("vocab", "dp"), P("dp", "vocab"))
    return jax.shard_map(
        functools.partial(per_device, mesh.shape["vocab"]),
        mesh=mesh,
        in_specs=in_specs,
        out_specs=out_specs,
        check_vma=False,
    )
```

```python
import functools

import jax
import jax.numpy as jnp
from jax import lax
from jax.experimental import pallas as pl
from jax.experimental.pallas import tpu as pltpu
from jax.sharding import PartitionSpec as P

F32 = jnp.float32
BF16 = jnp.bfloat16
I32 = jnp.int32
MESH = pl.DeviceIdType.MESH
SIDE = 4
LANES = 128
GROUPS = 2
ROWS = 8
FLOWS = ((0, 1), (0, -1), (1, 1), (1, -1))
LARGEST = 32766.0


def encode(blocks, dst):
    tiles = blocks[0].shape[1] // (2 * LANES)
    parts = []
    for block in blocks:
        for t in range(tiles):
            u = t + tiles
            parts.append(
                (block[:, t * LANES : (t + 1) * LANES], block[:, u * LANES : (u + 1) * LANES])
            )
    peak = jnp.full((ROWS, LANES), 1e-30, F32)
    for high, low in parts:
        peak = jnp.maximum(peak, jnp.maximum(jnp.abs(high), jnp.abs(low)))
    power = jnp.ceil(jnp.log2(peak) * 8.0)
    inverse = jnp.exp2(power * -0.125) * LARGEST
    for k, (high, low) in enumerate(parts):
        high_code = jnp.round(high * inverse).astype(I32)
        low_code = jnp.round(low * inverse).astype(I32)
        dst[:, k * LANES : (k + 1) * LANES] = (high_code << 16) | (low_code & 0xFFFF)
    end = len(parts) * LANES
    dst[:, end : end + LANES] = power.astype(I32)


def decode(src, block, width):
    end = src.shape[1] - LANES
    scale = jnp.exp2(src[:, end : end + LANES].astype(F32) * 0.125) * (1.0 / LARGEST)
    highs, lows = [], []
    for t in range(width // (2 * LANES)):
        start = block * (width // 2) + t * LANES
        word = src[:, start : start + LANES]
        highs.append((word >> 16).astype(F32) * scale)
        lows.append(((word << 16) >> 16).astype(F32) * scale)
    return jnp.concatenate(highs + lows, axis=1)


def head_kernel(
    vocab_count,
    hidden_hbm,
    weight_hbm,
    ref_hbm,
    target_hbm,
    owner_hbm,
    cot_lp_hbm,
    cot_kl_hbm,
    grads_out,
    rows_out,
    feature_out,
    tokens_out,
    hidden,
    ref,
    target_row,
    owner_row,
    cot_lp,
    cot_kl,
    rows,
    rows_turned,
    feature_result,
    tokens_result,
    weight,
    part,
    send1,
    recv1,
    send2,
    recv2,
    logits,
    grads,
    peaks,
    cots,
    stats,
    tokens,
    slots,
    ref32,
    core_recv,
    zsend,
    zrecv,
    in_sem,
    w_sem,
    rs_send,
    rs_recv,
    ag_send,
    ag_recv,
    st_send,
    st_recv,
    tk_send,
    tk_recv,
    core_send_sem,
    core_recv_sem,
    z_send,
    z_recv,
    out_sem,
    end_sem,
):
    width = weight.shape[2]
    rows_all = hidden.shape[0]
    count = owner_row.shape[1]
    chips = SIDE * SIDE
    rows_dev = count // chips
    levels = vocab_count // 2
    dp = lax.axis_index("dp")
    vocab = lax.axis_index("vocab")
    here = (dp // SIDE, dp % SIDE)
    level, core = vocab // 2, vocab % 2

    def along(axis, offset):
        return lax.rem(here[axis] + offset + SIDE, SIDE)

    def device(axis, offset):
        moved = along(axis, offset)
        return (moved * SIDE + here[1], vocab) if axis == 0 else (here[0] * SIDE + moved, vocab)

    def place(f, first, second):
        return (first, second) if FLOWS[f][0] == 0 else (second, first)

    barrier = pltpu.get_barrier_semaphore()
    for axis in range(2):
        for step in range(1, SIDE):
            pl.semaphore_signal(barrier, inc=1, device_id=device(axis, step), device_id_type=MESH)
    for step in range(1, vocab_count):
        pl.semaphore_signal(
            barrier, inc=1, device_id=(dp, (vocab + step) % vocab_count), device_id_type=MESH
        )
    greeted = 2 * (SIDE - 1) + vocab_count - 1

    inputs = [
        pltpu.make_async_copy(source, landing, in_sem.at[k])
        for k, (source, landing) in enumerate(
            (
                (owner_hbm, owner_row),
                (hidden_hbm, hidden),
                (cot_lp_hbm, cot_lp),
                (cot_kl_hbm, cot_kl),
                (target_hbm, target_row),
                (ref_hbm, ref),
            )
        )
    ]
    for copy in inputs:
        copy.start()

    def weight_copy(f):
        cols = pl.ds(f * width, width)
        return pltpu.make_async_copy(weight_hbm.at[:, cols], weight.at[f], w_sem.at[f])

    for f in range(4):
        weight_copy(f).start()

    def iota(shape, dim):
        return lax.broadcasted_iota(I32, shape, dim)

    inputs[0].wait()
    rows_i, cols_i = iota((count, count), 0), iota((count, count), 1)
    diagonal = rows_i == cols_i

    def turned(row):
        return jnp.sum(jnp.where(diagonal, row, 0), axis=1, keepdims=True)

    owner_col = turned(owner_row[...].astype(F32)).astype(I32)
    alike = (owner_col == owner_row[...]) & (rows_i // rows_dev == cols_i // rows_dev)
    before_col = jnp.sum(jnp.where(alike & (cols_i < rows_i), 1.0, 0.0), axis=1, keepdims=True)
    before_row = jnp.sum(jnp.where(alike & (rows_i < cols_i), 1.0, 0.0), axis=0, keepdims=True)
    slot_count = rows_all // chips
    capacity = slot_count // chips
    slot_col = (
        owner_col * slot_count
        + (iota((count, 1), 0) // rows_dev) * capacity
        + before_col.astype(I32)
    )
    slot_row = (
        owner_row[...] * slot_count
        + (iota((1, count), 1) // rows_dev) * capacity
        + before_row.astype(I32)
    )
    placing = slot_col == iota((count, rows_all), 1)
    inputs[1].wait()
    rows[...] = jnp.dot(
        jnp.where(placing, 1.0, 0.0).astype(BF16), hidden[...], preferred_element_type=F32
    ).astype(BF16)

    def rs_copy(s, f, kind):
        axis, way = FLOWS[f]
        stage, role = kind // 3, kind % 3
        if stage == 1:
            axis = 1 - axis
        source, landing = (send1, recv1) if stage == 0 else (send2, recv2)
        return pltpu.make_async_remote_copy(
            src_ref=source.at[s, f, role],
            dst_ref=landing.at[s, f, role],
            send_sem=rs_send.at[s, stage],
            recv_sem=rs_recv.at[s, kind],
            device_id=device(axis, -way if role == 1 else way),
            device_id_type=MESH,
        )

    def rs_arrived(s, kind):
        landing = (recv1, recv2)[kind // 3].at[s, :, kind % 3]
        pltpu.make_async_copy(landing, landing, rs_recv.at[s, kind]).wait()

    def first_blocks(s, f, offset):
        first = along(FLOWS[f][0], offset)
        return [part[(s, f) + place(f, first, k)] for k in range(SIDE)]

    def second_block(s, f, offset):
        axis = FLOWS[f][0]
        return part[(s, f) + place(f, here[axis], along(1 - axis, offset))]

    def multiply(f):
        weight_copy(f).wait()
        product = jnp.dot(rows[...], weight[f], preferred_element_type=F32)
        product = product.reshape(SIDE, SIDE, rows_dev, width)
        part[0, f] = product[:, :, 0:ROWS]
        part[1, f] = product[:, :, ROWS:rows_dev]

    def first_ahead(s, f):
        encode(first_blocks(s, f, 2), send1.at[s, f, 0])
        rs_copy(s, f, 0).start()

    def first_back(s, f):
        encode(first_blocks(s, f, -FLOWS[f][1]), send1.at[s, f, 1])
        rs_copy(s, f, 1).start()

    def first_relay(s):
        rs_arrived(s, 0)
        for f in range(4):
            own = first_blocks(s, f, FLOWS[f][1])
            arrived = recv1.at[s, f, 0]
            encode(
                [own[k] + decode(arrived, k, width) for k in range(SIDE)], send1.at[s, f, 2]
            )
        for f in range(4):
            rs_copy(s, f, 2).start()

    def first_sum(s):
        rs_arrived(s, 1)
        rs_arrived(s, 2)
        for f in range(4):
            axis, way = FLOWS[f]
            for k in range(SIDE):
                spot = (s, f) + place(f, here[axis], k)
                part[spot] = (
                    part[spot]
                    + decode(recv1.at[s, f, 1], k, width)
                    + decode(recv1.at[s, f, 2], k, width)
                )
        for f in range(4):
            way = FLOWS[f][1]
            encode([second_block(s, f, 2)], send2.at[s, f, 0])
            encode([second_block(s, f, -way)], send2.at[s, f, 1])
        for f in range(4):
            rs_copy(s, f, 3).start()
            rs_copy(s, f, 4).start()

    def second_relay(s):
        rs_arrived(s, 3)
        for f in range(4):
            encode(
                [second_block(s, f, FLOWS[f][1]) + decode(recv2.at[s, f, 0], 0, width)],
                send2.at[s, f, 2],
            )
        for f in range(4):
            rs_copy(s, f, 5).start()

    def second_sum(s):
        rs_arrived(s, 4)
        rs_arrived(s, 5)
        peak = jnp.full((ROWS, LANES), -jnp.inf, F32)
        for f in range(4):
            done = (
                second_block(s, f, 0)
                + decode(recv2.at[s, f, 1], 0, width)
                + decode(recv2.at[s, f, 2], 0, width)
            )
            logits[s, f] = done
            for t in range(width // LANES):
                peak = jnp.maximum(peak, done[:, t * LANES : (t + 1) * LANES])
        peaks[s] = peak

    def ref_piece(s, f):
        return ref32[s * ROWS : (s + 1) * ROWS, f * width : (f + 1) * width]

    def lane_sum(values):
        total = values[:, 0:LANES]
        for t in range(1, width // LANES):
            total = total + values[:, t * LANES : (t + 1) * LANES]
        return total

    first_col = vocab * (4 * width)
    lane = iota((ROWS, LANES), 1)

    def my_cots(s):
        start = pl.multiple_of(dp * rows_dev, rows_dev) + s * ROWS
        mine = cots[pl.ds(pl.multiple_of(start, ROWS), ROWS), :]
        return mine[:, 0:1], mine[:, 1:2], mine[:, 2:3].astype(I32)

    def hit(f, target):
        return first_col + f * width + iota((ROWS, width), 1) == target

    def ref_stats(s):
        peak = jnp.full((ROWS, 1), -jnp.inf, F32)
        for f in range(4):
            peak = jnp.maximum(peak, jnp.max(ref_piece(s, f), axis=1, keepdims=True))
        mass = jnp.zeros((ROWS, LANES), F32)
        for f in range(4):
            mass = mass + lane_sum(jnp.exp(ref_piece(s, f) - peak))
        return peak, jnp.sum(mass, axis=1, keepdims=True)

    def stats_copy(s, step):
        return pltpu.make_async_remote_copy(
            src_ref=stats.at[s, vocab],
            dst_ref=stats.at[s, vocab],
            send_sem=st_send.at[s],
            recv_sem=st_recv.at[s],
            device_id=(dp, (vocab + step) % vocab_count),
            device_id_type=MESH,
        )

    def stats_send(s, ref_side):
        target = my_cots(s)[2]
        peak = jnp.max(peaks[s], axis=1, keepdims=True)
        mass = cross = picked = jnp.zeros((ROWS, LANES), F32)
        for f in range(4):
            values = logits[s, f]
            weights = jnp.exp(values - peak)
            mass = mass + lane_sum(weights)
            cross = cross + lane_sum(weights * (values - ref_piece(s, f)))
            picked = picked + lane_sum(jnp.where(hit(f, target), values, 0.0))
        mass, cross, picked = [
            jnp.sum(value, axis=1, keepdims=True) for value in (mass, cross, picked)
        ]
        packed = jnp.zeros((ROWS, LANES), F32)
        for k, value in enumerate((peak, mass, cross) + ref_side + (picked,)):
            packed = packed + jnp.where(lane == k, value, 0.0)
        stats[s, vocab] = packed
        for step in range(1, vocab_count):
            stats_copy(s, step).start()

    def other_stats(s):
        return stats.at[s, pl.ds(0, vocab_count - 1)]

    def stats_finish(s):
        pltpu.make_async_copy(other_stats(s), other_stats(s), st_recv.at[s]).wait()
        every = [stats[s, k] for k in range(vocab_count)]
        peak, ref_peak = every[0][:, 0:1], every[0][:, 3:4]
        for tile in every[1:]:
            peak = jnp.maximum(peak, tile[:, 0:1])
            ref_peak = jnp.maximum(ref_peak, tile[:, 3:4])
        mass, cross, ref_mass, picked = 0.0, 0.0, 0.0, 0.0
        for tile in every:
            scale = jnp.exp(tile[:, 0:1] - peak)
            mass = mass + tile[:, 1:2] * scale
            cross = cross + tile[:, 2:3] * scale
            ref_mass = ref_mass + tile[:, 4:5] * jnp.exp(tile[:, 3:4] - ref_peak)
            picked = picked + tile[:, 5:6]
        norm = peak + jnp.log(mass)
        ref_norm = ref_peak + jnp.log(ref_mass)
        row_kl = cross / mass - norm + ref_norm
        tokens[here[0], here[1], s * ROWS : (s + 1) * ROWS] = (
            jnp.where(lane == 0, picked - norm, 0.0)
            + jnp.where(lane == 1, row_kl, 0.0)
            + jnp.where(lane == 2, norm, 0.0)
        )
        return norm, ref_norm - norm - row_kl

    half = width // 2

    def gradients(s, norm, shift):
        lp, kl, target = my_cots(s)
        for f in range(4):
            values = logits[s, f]
            probs = jnp.exp(values - norm)
            excess = values - ref_piece(s, f) + shift
            result = jnp.where(hit(f, target), lp, 0.0) + probs * (kl * excess - lp)
            result = jnp.concatenate([result[:, 0:half], result[:, half:width]], axis=0)
            grads[s, f, here[0], here[1]] = result.astype(BF16)

    def relay_copy(buffer, f, kind, send_sem, recv_sem):
        axis, way = FLOWS[f]
        other = 1 - axis
        if kind < 3:
            spot = place(f, along(axis, -way if kind == 2 else 0), here[other])
            to = device(axis, -way if kind == 1 else way)
        else:
            spot = place(f, slice(None), along(other, -way if kind == 5 else 0))
            to = device(other, -way if kind == 4 else way)
        block = buffer.at[spot]
        return pltpu.make_async_remote_copy(
            src_ref=block,
            dst_ref=block,
            send_sem=send_sem,
            recv_sem=recv_sem,
            device_id=to,
            device_id_type=MESH,
        )

    def ag_copy(g, f, kind):
        return relay_copy(grads.at[g, f], f, kind, ag_send.at[g, kind // 3], ag_recv.at[g, kind])

    def ag_go(g, kinds):
        for kind in kinds:
            for f in range(4):
                ag_copy(g, f, kind).start()

    def ag_arrived(g, kinds):
        for kind in kinds:
            landing = grads.at[g, 0] if kind >= 3 else grads.at[g, 0, 0]
            pltpu.make_async_copy(landing, landing, ag_recv.at[g, kind]).wait()

    def tokens_copy(axis, step):
        block = tokens.at[here] if axis == 1 else tokens.at[here[0]]
        return pltpu.make_async_remote_copy(
            src_ref=block,
            dst_ref=block,
            send_sem=tk_send.at[axis],
            recv_sem=tk_recv.at[axis],
            device_id=device(axis, step),
            device_id_type=MESH,
        )

    def tokens_go(axis):
        for step in range(1, SIDE):
            tokens_copy(axis, step).start()

    def tokens_moved(axis, sem):
        moved = tokens.at[0, pl.ds(0, 3)] if axis == 1 else tokens.at[pl.ds(0, 3)]
        pltpu.make_async_copy(moved, moved, sem.at[axis]).wait()

    def out_copy(g, f):
        return pltpu.make_async_copy(grads.at[g, f], grads_out.at[g, f], out_sem.at[g, f])

    def group_token(g, shape, dim):
        order = iota(shape, dim)
        return (order // ROWS) * rows_dev + g * ROWS + lax.rem(order, ROWS)

    members = count // GROUPS

    def spread(g):
        shape = (count, members)
        chosen = iota(shape, 0) == group_token(g, shape, 1)
        slot_of = jnp.sum(jnp.where(chosen, slot_col.astype(F32), 0.0), axis=0, keepdims=True)
        matches = iota((rows_all, members), 0) == slot_of.astype(I32)
        return jnp.where(matches, 1.0, 0.0).astype(BF16)

    def feature_step(g):
        for f in range(4):
            out_copy(g, f).start()
        total = jnp.zeros((members, rows.shape[1]), F32)
        for f in range(4):
            for h in range(2):
                piece = grads[g, f, :, :, h * ROWS : (h + 1) * ROWS, :].reshape(members, half)
                total = total + lax.dot_general(
                    piece,
                    weight[f, :, h * half : (h + 1) * half],
                    (((1,), (1,)), ((), ())),
                    preferred_element_type=F32,
                )
        to_slots = spread(g)
        high = total.astype(BF16)
        rest = total - high.astype(F32)
        middle = rest.astype(BF16)
        low = (rest - middle.astype(F32)).astype(BF16)
        placed = jnp.dot(to_slots, high, preferred_element_type=F32)
        placed = placed + jnp.dot(to_slots, middle, preferred_element_type=F32)
        placed = placed + jnp.dot(to_slots, low, preferred_element_type=F32)
        return placed.reshape(slots.shape)

    for f in range(4):
        multiply(f)
        if f == 0:
            pl.semaphore_wait(barrier, greeted)
        first_ahead(0, f)
    for f in range(4):
        first_back(0, f)
    for copy in inputs[2:]:
        copy.wait()
    ref32[...] = ref[...].astype(F32)
    lp_col = jnp.sum(jnp.where(placing, cot_lp[...], 0.0), axis=1, keepdims=True)
    kl_col = jnp.sum(jnp.where(placing, cot_kl[...], 0.0), axis=1, keepdims=True)
    target_col = turned(target_row[...].astype(F32))
    lane_all = iota((count, LANES), 1)
    cots[...] = (
        jnp.where(lane_all == 0, lp_col, 0.0)
        + jnp.where(lane_all == 1, kl_col, 0.0)
        + jnp.where(lane_all == 2, target_col, 0.0)
    )
    first_relay(0)
    for f in range(4):
        first_ahead(1, f)
    for f in range(4):
        first_back(1, f)
    ref_side = [ref_stats(0), ref_stats(1)]
    for g in range(GROUPS):
        rows_turned[:, g * members : (g + 1) * members] = lax.dot_general(
            hidden[...], spread(g), (((0,), (0,)), ((), ())), preferred_element_type=F32
        ).astype(BF16)
    rows_copy = pltpu.make_async_copy(rows_turned, rows_out, end_sem.at[0])
    rows_copy.start()
    first_sum(0)
    first_relay(1)
    second_relay(0)
    first_sum(1)
    second_sum(0)
    stats_send(0, ref_side[0])
    second_relay(1)
    gradients(0, *stats_finish(0))
    ag_go(0, (0, 1))
    second_sum(1)
    stats_send(1, ref_side[1])
    ag_arrived(0, (0,))
    ag_go(0, (2,))
    gradients(1, *stats_finish(1))
    ag_go(1, (0, 1))
    tokens_go(1)
    ag_arrived(0, (1, 2))
    ag_go(0, (3, 4))
    ag_arrived(1, (0,))
    ag_go(1, (2,))
    ag_arrived(1, (1, 2))
    ag_go(1, (3, 4))
    ag_arrived(0, (3,))
    ag_go(0, (5,))
    ag_arrived(1, (3,))
    ag_go(1, (5,))
    tokens_moved(1, tk_recv)
    tokens_go(0)
    ag_arrived(0, (4, 5))
    slots[...] = feature_step(0)
    ag_arrived(1, (4, 5))
    slots[...] = slots[...] + feature_step(1)

    core_copy = pltpu.make_async_remote_copy(
        src_ref=slots.at[:, 1 - core],
        dst_ref=core_recv,
        send_sem=core_send_sem,
        recv_sem=core_recv_sem,
        device_id=(dp, level * 2 + 1 - core),
        device_id_type=MESH,
    )
    core_copy.start()

    tokens_moved(0, tk_recv)
    everyone = tokens[...].reshape(count, LANES)
    mine_slots = slot_col == dp * slot_count + lane_all
    mine_slots = mine_slots & (lane_all < slot_count)
    for k in range(3):
        tokens_result[k : k + 1, :] = jnp.sum(
            jnp.where(mine_slots, everyone[:, k : k + 1], 0.0), axis=0, keepdims=True
        )

    tokens_copied = pltpu.make_async_copy(tokens_result, tokens_out, end_sem.at[1])
    tokens_copied.start()
    core_copy.wait_recv()
    slot_rows = slots.shape[2]
    feature_width = slots.shape[3]

    def pair_sum(l):
        return slots[l, core] + core_recv[l]

    def z_copy(step):
        return pltpu.make_async_remote_copy(
            src_ref=zsend.at[step],
            dst_ref=zrecv.at[step],
            send_sem=z_send.at[step],
            recv_sem=z_recv.at[step],
            device_id=(dp, ((level + step) % levels) * 2 + core),
            device_id_type=MESH,
        )

    for step in (2, 1, 3):
        if step < levels:
            both = pair_sum((level + step) % levels)
            encode([both[k : k + ROWS] for k in range(0, slot_rows, ROWS)], zsend.at[step])
            z_copy(step).start()
    total = pair_sum(level)
    for step in range(1, levels):
        z_copy(step).wait_recv()
    pieces_out = []
    for k in range(slot_rows // ROWS):
        block = total[k * ROWS : (k + 1) * ROWS]
        for step in range(1, levels):
            block = block + decode(zrecv.at[step], k, feature_width)
        pieces_out.append(block)
    feature_result[...] = jnp.concatenate(pieces_out, axis=0).astype(BF16)
    feature_copied = pltpu.make_async_copy(feature_result, feature_out, end_sem.at[2])
    feature_copied.start()

    def left(source, sem):
        pltpu.make_async_copy(source, source, sem).wait()

    for s in range(GROUPS):
        left(send1.at[s], rs_send.at[s, 0])
        left(send2.at[s], rs_send.at[s, 1])
    for g in range(GROUPS):
        left(grads.at[g, :, 0, pl.ds(0, 3)], ag_send.at[g, 0])
        left(grads.at[g, pl.ds(0, 3)], ag_send.at[g, 1])
        for f in range(4):
            out_copy(g, f).wait()
        left(other_stats(g), st_send.at[g])
    for axis in range(2):
        tokens_moved(axis, tk_send)
    core_copy.wait_send()
    for step in range(1, levels):
        z_copy(step).wait_send()
    rows_copy.wait()
    tokens_copied.wait()
    feature_copied.wait()


def weight_kernel(
    rows_in,
    grads_in,
    feature_in,
    tokens_in,
    out,
    feature_out,
    first,
    second,
    third,
    rows,
    grads,
    tokens,
    small,
    result,
    in_sem,
    out_sem,
):
    width = grads.shape[5]
    members = rows.shape[1] // GROUPS

    def load(f):
        return pltpu.make_async_copy(grads_in.at[:, f], grads.at[f], in_sem.at[f])

    def store(f, h):
        cols = pl.ds((2 * f + h) * width, width)
        return pltpu.make_async_copy(result.at[f, h], out.at[:, cols], out_sem.at[f, h])

    rows_copy = pltpu.make_async_copy(rows_in, rows, in_sem.at[4])
    rows_copy.start()
    for f in range(4):
        load(f).start()
    tokens_copy = pltpu.make_async_copy(tokens_in, tokens, in_sem.at[5])
    tokens_copy.start()
    feature_copy = pltpu.make_async_copy(feature_in, feature_out, in_sem.at[6])
    feature_copy.start()
    rows_copy.wait()
    for f in range(4):
        load(f).wait()
        for h in range(2):
            total = 0.0
            for g in range(GROUPS):
                piece = grads[f, g, :, :, h * ROWS : (h + 1) * ROWS, :].reshape(members, width)
                total = total + jnp.dot(
                    rows[:, g * members : (g + 1) * members], piece, preferred_element_type=F32
                )
            result[f, h] = total.astype(BF16)
            store(f, h).start()
    tokens_copy.wait()
    outs = []
    for k, token_out in enumerate((first, second, third)):
        small[k] = tokens[k : k + 1, 0 : small.shape[2]]
        outs.append(pltpu.make_async_copy(small.at[k], token_out, in_sem.at[7 + k]))
        outs[-1].start()
    feature_copy.wait()
    for copy in outs:
        copy.wait()
    for f in range(4):
        for h in range(2):
            store(f, h).wait()


def per_device(
    vocab_count, pol_hidden, pol_weight, ref_logits, targets, owners, grad_logprob, grad_kl
):
    all_slots, depth = pol_hidden.shape
    cols = pol_weight.shape[1]
    rows_dev = ref_logits.shape[0]
    count = owners.shape[0]
    chips = SIDE * SIDE
    width = cols // 4
    slot_count = all_slots // chips
    levels = vocab_count // 2
    slot_rows = all_slots // vocab_count
    unit1 = (GROUPS, 4, 3, ROWS, SIDE * width // 2 + LANES)
    unit2 = (GROUPS, 4, 3, ROWS, width // 2 + LANES)
    unit3 = (levels, ROWS, slot_rows // ROWS * depth // 2 + LANES)
    grads_shape = (GROUPS, 4, SIDE, SIDE, rows_dev, width // 2)
    anywhere = pl.BlockSpec(memory_space=pl.ANY)
    flops = 2 * count * depth * cols * 2
    grads, rows, feature, tokens = pl.pallas_call(
        functools.partial(head_kernel, vocab_count),
        out_shape=(
            jax.ShapeDtypeStruct(grads_shape, BF16),
            jax.ShapeDtypeStruct((depth, count), BF16),
            jax.ShapeDtypeStruct((slot_rows, depth), BF16),
            jax.ShapeDtypeStruct((8, LANES), F32),
        ),
        in_specs=[pl.BlockSpec(memory_space=pltpu.HBM)] * 7,
        out_specs=(anywhere,) * 4,
        scratch_shapes=[
            pltpu.VMEM((all_slots, depth), BF16),
            pltpu.VMEM((rows_dev, cols), BF16),
            pltpu.VMEM((1, count), I32),
            pltpu.VMEM((1, count), I32),
            pltpu.VMEM((1, all_slots), F32),
            pltpu.VMEM((1, all_slots), F32),
            pltpu.VMEM((count, depth), BF16),
            pltpu.VMEM((depth, count), BF16),
            pltpu.VMEM((slot_rows, depth), BF16),
            pltpu.VMEM((8, LANES), F32),
            pltpu.VMEM((4, depth, width), BF16),
            pltpu.VMEM((GROUPS, 4, SIDE, SIDE, ROWS, width), F32),
            pltpu.VMEM(unit1, I32),
            pltpu.VMEM(unit1, I32),
            pltpu.VMEM(unit2, I32),
            pltpu.VMEM(unit2, I32),
            pltpu.VMEM((GROUPS, 4, ROWS, width), F32),
            pltpu.VMEM(grads_shape, BF16),
            pltpu.VMEM((GROUPS, ROWS, LANES), F32),
            pltpu.VMEM((count, LANES), F32),
            pltpu.VMEM((GROUPS, vocab_count, ROWS, LANES), F32),
            pltpu.VMEM((SIDE, SIDE, rows_dev, LANES), F32),
            pltpu.VMEM((levels, 2, slot_rows, depth), F32),
            pltpu.VMEM((rows_dev, cols), F32),
            pltpu.VMEM((levels, slot_rows, depth), F32),
            pltpu.VMEM(unit3, I32),
            pltpu.VMEM(unit3, I32),
            pltpu.SemaphoreType.DMA((6,)),
            pltpu.SemaphoreType.DMA((4,)),
            pltpu.SemaphoreType.DMA((GROUPS, 2)),
            pltpu.SemaphoreType.DMA((GROUPS, 6)),
            pltpu.SemaphoreType.DMA((GROUPS, 2)),
            pltpu.SemaphoreType.DMA((GROUPS, 6)),
            pltpu.SemaphoreType.DMA((GROUPS,)),
            pltpu.SemaphoreType.DMA((GROUPS,)),
            pltpu.SemaphoreType.DMA((2,)),
            pltpu.SemaphoreType.DMA((2,)),
            pltpu.SemaphoreType.DMA,
            pltpu.SemaphoreType.DMA,
            pltpu.SemaphoreType.DMA((levels,)),
            pltpu.SemaphoreType.DMA((levels,)),
            pltpu.SemaphoreType.DMA((GROUPS, 4)),
            pltpu.SemaphoreType.DMA((3,)),
        ],
        compiler_params=pltpu.CompilerParams(
            collective_id=0, has_side_effects=True, vmem_limit_bytes=60 * 2**20
        ),
        cost_estimate=pl.CostEstimate(
            flops=flops, bytes_accessed=3 * depth * cols, transcendentals=3 * rows_dev * cols
        ),
        name="head",
    )(
        pol_hidden,
        pol_weight,
        ref_logits,
        targets.reshape(1, count),
        owners.reshape(1, count),
        grad_logprob.reshape(1, all_slots),
        grad_kl.reshape(1, all_slots),
    )
    token_shape = jax.ShapeDtypeStruct((1, slot_count), F32)
    weight_grad, feature, first, second, third = pl.pallas_call(
        weight_kernel,
        out_shape=(
            jax.ShapeDtypeStruct((depth, cols), BF16),
            jax.ShapeDtypeStruct((slot_rows, depth), BF16),
            token_shape,
            token_shape,
            token_shape,
        ),
        in_specs=[anywhere] * 4,
        out_specs=(anywhere,) * 5,
        scratch_shapes=[
            pltpu.VMEM((depth, count), BF16),
            pltpu.VMEM((4, GROUPS) + grads_shape[2:], BF16),
            pltpu.VMEM((8, LANES), F32),
            pltpu.VMEM((3, 1, slot_count), F32),
            pltpu.VMEM((4, 2, depth, width // 2), BF16),
            pltpu.SemaphoreType.DMA((10,)),
            pltpu.SemaphoreType.DMA((4, 2)),
        ],
        compiler_params=pltpu.CompilerParams(vmem_limit_bytes=60 * 2**20),
        cost_estimate=pl.CostEstimate(
            flops=2 * count * depth * cols,
            bytes_accessed=2 * (depth + count) * cols,
            transcendentals=0,
        ),
        name="weight_grad",
    )(rows, grads, feature, tokens)
    return (
        first.reshape(slot_count),
        second.reshape(slot_count),
        third.reshape(slot_count),
        feature,
        weight_grad,
    )


def solution(mesh):
    in_specs = (P(None, "dp"), P("dp", "vocab"), P("dp", "vocab"), P(), P(), P(), P())
    out_specs = (P("dp"), P("dp"), P("dp"), P("vocab", "dp"), P("dp", "vocab"))
    return jax.shard_map(
        functools.partial(per_device, mesh.shape["vocab"]),
        mesh=mesh,
        in_specs=in_specs,
        out_specs=out_specs,
        check_vma=False,
    )
```

```python
import functools

import jax
import jax.numpy as jnp
from jax import lax
from jax.experimental import pallas as pl
from jax.experimental.pallas import tpu as pltpu
from jax.sharding import PartitionSpec as P

F32 = jnp.float32
BF16 = jnp.bfloat16
I32 = jnp.int32
MESH = pl.DeviceIdType.MESH
SIDE = 4
LANES = 128
GROUPS = 2
ROWS = 8
FLOWS = ((0, 1), (0, -1), (1, 1), (1, -1))
ORDER = (0, 2, 1, 3)
LARGEST = 32766.0


def encode(blocks, dst):
    tiles = blocks[0].shape[1] // (2 * LANES)
    parts = []
    for block in blocks:
        for t in range(tiles):
            u = t + tiles
            parts.append(
                (block[:, t * LANES : (t + 1) * LANES], block[:, u * LANES : (u + 1) * LANES])
            )
    peak = jnp.full((ROWS, LANES), 1e-30, F32)
    for high, low in parts:
        peak = jnp.maximum(peak, jnp.maximum(jnp.abs(high), jnp.abs(low)))
    power = jnp.ceil(jnp.log2(peak) * 8.0)
    inverse = jnp.exp2(power * -0.125) * LARGEST
    for k, (high, low) in enumerate(parts):
        high_code = jnp.round(high * inverse).astype(I32)
        low_code = jnp.round(low * inverse).astype(I32)
        dst[:, k * LANES : (k + 1) * LANES] = (high_code << 16) | (low_code & 0xFFFF)
    end = len(parts) * LANES
    dst[:, end : end + LANES] = power.astype(I32)


def decode(src, block, width):
    end = src.shape[1] - LANES
    scale = jnp.exp2(src[:, end : end + LANES].astype(F32) * 0.125) * (1.0 / LARGEST)
    highs, lows = [], []
    for t in range(width // (2 * LANES)):
        start = block * (width // 2) + t * LANES
        word = src[:, start : start + LANES]
        highs.append((word >> 16).astype(F32) * scale)
        lows.append(((word << 16) >> 16).astype(F32) * scale)
    return jnp.concatenate(highs + lows, axis=1)


def head_kernel(
    vocab_count,
    hidden_hbm,
    weight_hbm,
    ref_hbm,
    target_hbm,
    owner_hbm,
    cot_lp_hbm,
    cot_kl_hbm,
    grads_out,
    rows_out,
    feature_out,
    tokens_out,
    hidden,
    ref,
    target_row,
    owner_row,
    cot_lp,
    cot_kl,
    rows,
    rows_turned,
    feature_result,
    tokens_result,
    weight,
    part,
    send1,
    recv1,
    send2,
    recv2,
    logits,
    grads,
    peaks,
    cots,
    stats,
    tokens,
    slots,
    ref32,
    core_recv,
    zsend,
    zrecv,
    in_sem,
    w_sem,
    rs_send,
    rs_recv,
    ag_send,
    ag_recv,
    st_send,
    st_recv,
    tk_send,
    tk_recv,
    core_send_sem,
    core_recv_sem,
    z_send,
    z_recv,
    out_sem,
    end_sem,
):
    width = weight.shape[2]
    rows_all = hidden.shape[0]
    count = owner_row.shape[1]
    chips = SIDE * SIDE
    rows_dev = count // chips
    levels = vocab_count // 2
    dp = lax.axis_index("dp")
    vocab = lax.axis_index("vocab")
    here = (dp // SIDE, dp % SIDE)
    level, core = vocab // 2, vocab % 2

    def along(axis, offset):
        return lax.rem(here[axis] + offset + SIDE, SIDE)

    def device(axis, offset):
        moved = along(axis, offset)
        return (moved * SIDE + here[1], vocab) if axis == 0 else (here[0] * SIDE + moved, vocab)

    def place(f, first, second):
        return (first, second) if FLOWS[f][0] == 0 else (second, first)

    barrier = pltpu.get_barrier_semaphore()
    for axis in range(2):
        for step in range(1, SIDE):
            pl.semaphore_signal(barrier, inc=1, device_id=device(axis, step), device_id_type=MESH)
    for step in range(1, vocab_count):
        pl.semaphore_signal(
            barrier, inc=1, device_id=(dp, (vocab + step) % vocab_count), device_id_type=MESH
        )
    greeted = 2 * (SIDE - 1) + vocab_count - 1

    inputs = [
        pltpu.make_async_copy(source, landing, in_sem.at[k])
        for k, (source, landing) in enumerate(
            (
                (owner_hbm, owner_row),
                (hidden_hbm, hidden),
                (cot_lp_hbm, cot_lp),
                (cot_kl_hbm, cot_kl),
                (target_hbm, target_row),
                (ref_hbm, ref),
            )
        )
    ]
    for copy in inputs:
        copy.start()

    def weight_copy(f):
        cols = pl.ds(f * width, width)
        return pltpu.make_async_copy(weight_hbm.at[:, cols], weight.at[f], w_sem.at[f])

    for f in range(4):
        weight_copy(f).start()

    def iota(shape, dim):
        return lax.broadcasted_iota(I32, shape, dim)

    inputs[0].wait()
    rows_i, cols_i = iota((count, count), 0), iota((count, count), 1)
    diagonal = rows_i == cols_i

    def turned(row):
        return jnp.sum(jnp.where(diagonal, row, 0), axis=1, keepdims=True)

    owner_col = turned(owner_row[...].astype(F32)).astype(I32)
    alike = (owner_col == owner_row[...]) & (rows_i // rows_dev == cols_i // rows_dev)
    before_col = jnp.sum(jnp.where(alike & (cols_i < rows_i), 1.0, 0.0), axis=1, keepdims=True)
    before_row = jnp.sum(jnp.where(alike & (rows_i < cols_i), 1.0, 0.0), axis=0, keepdims=True)
    slot_count = rows_all // chips
    capacity = slot_count // chips
    slot_col = (
        owner_col * slot_count
        + (iota((count, 1), 0) // rows_dev) * capacity
        + before_col.astype(I32)
    )
    slot_row = (
        owner_row[...] * slot_count
        + (iota((1, count), 1) // rows_dev) * capacity
        + before_row.astype(I32)
    )
    placing = slot_col == iota((count, rows_all), 1)
    inputs[1].wait()
    rows[...] = jnp.dot(
        jnp.where(placing, 1.0, 0.0).astype(BF16), hidden[...], preferred_element_type=F32
    ).astype(BF16)

    def rs_copy(s, f, kind):
        axis, way = FLOWS[f]
        stage, role = kind // 3, kind % 3
        if stage == 1:
            axis = 1 - axis
        source, landing = (send1, recv1) if stage == 0 else (send2, recv2)
        return pltpu.make_async_remote_copy(
            src_ref=source.at[s, f, role],
            dst_ref=landing.at[s, f, role],
            send_sem=rs_send.at[s, stage],
            recv_sem=rs_recv.at[s, kind, f],
            device_id=device(axis, 2 if kind == 3 else -way if role == 1 else way),
            device_id_type=MESH,
        )

    def first_blocks(s, f, offset):
        first = along(FLOWS[f][0], offset)
        return [part[(s, f) + place(f, first, k)] for k in range(SIDE)]

    def second_block(s, f, offset):
        axis = FLOWS[f][0]
        return part[(s, f) + place(f, here[axis], along(1 - axis, offset))]

    def multiply(f):
        weight_copy(f).wait()
        product = jnp.dot(rows[...], weight[f], preferred_element_type=F32)
        product = product.reshape(SIDE, SIDE, rows_dev, width)
        part[0, f] = product[:, :, 0:ROWS]
        part[1, f] = product[:, :, ROWS:rows_dev]

    def first_ahead(s, f):
        encode(first_blocks(s, f, 2), send1.at[s, f, 0])
        rs_copy(s, f, 0).start()

    def first_back(s, f):
        encode(first_blocks(s, f, -FLOWS[f][1]), send1.at[s, f, 1])
        rs_copy(s, f, 1).start()

    def first_relay(s):
        for f in ORDER:
            rs_copy(s, f, 0).wait_recv()
            own = first_blocks(s, f, FLOWS[f][1])
            arrived = recv1.at[s, f, 0]
            encode(
                [own[k] + decode(arrived, k, width) for k in range(SIDE)], send1.at[s, f, 2]
            )
            rs_copy(s, f, 2).start()

    def first_sum(s):
        for f in ORDER:
            rs_copy(s, f, 1).wait_recv()
            rs_copy(s, f, 2).wait_recv()
            axis, way = FLOWS[f]
            for k in range(SIDE):
                spot = (s, f) + place(f, here[axis], k)
                part[spot] = (
                    part[spot]
                    + decode(recv1.at[s, f, 1], k, width)
                    + decode(recv1.at[s, f, 2], k, width)
                )
            for role, offset in ((0, 2), (1, -way), (2, way)):
                encode([second_block(s, f, offset)], send2.at[s, f, role])
                rs_copy(s, f, 3 + role).start()

    def second_sum(s):
        peak = jnp.full((ROWS, LANES), -jnp.inf, F32)
        for f in ORDER:
            for kind in (3, 4, 5):
                rs_copy(s, f, kind).wait_recv()
            done = (
                second_block(s, f, 0)
                + decode(recv2.at[s, f, 0], 0, width)
                + decode(recv2.at[s, f, 1], 0, width)
                + decode(recv2.at[s, f, 2], 0, width)
            )
            logits[s, f] = done
            for t in range(width // LANES):
                peak = jnp.maximum(peak, done[:, t * LANES : (t + 1) * LANES])
        peaks[s] = peak

    def ref_piece(s, f):
        return ref32[s * ROWS : (s + 1) * ROWS, f * width : (f + 1) * width]

    def lane_sum(values):
        total = values[:, 0:LANES]
        for t in range(1, width // LANES):
            total = total + values[:, t * LANES : (t + 1) * LANES]
        return total

    first_col = vocab * (4 * width)
    lane = iota((ROWS, LANES), 1)

    def my_cots(s):
        start = pl.multiple_of(dp * rows_dev, rows_dev) + s * ROWS
        mine = cots[pl.ds(pl.multiple_of(start, ROWS), ROWS), :]
        return mine[:, 0:1], mine[:, 1:2], mine[:, 2:3].astype(I32)

    def hit(f, target):
        return first_col + f * width + iota((ROWS, width), 1) == target

    def ref_stats(s):
        peak = jnp.full((ROWS, 1), -jnp.inf, F32)
        for f in range(4):
            peak = jnp.maximum(peak, jnp.max(ref_piece(s, f), axis=1, keepdims=True))
        mass = jnp.zeros((ROWS, LANES), F32)
        for f in range(4):
            mass = mass + lane_sum(jnp.exp(ref_piece(s, f) - peak))
        return peak, jnp.sum(mass, axis=1, keepdims=True)

    def stats_copy(s, step):
        return pltpu.make_async_remote_copy(
            src_ref=stats.at[s, vocab],
            dst_ref=stats.at[s, vocab],
            send_sem=st_send.at[s],
            recv_sem=st_recv.at[s],
            device_id=(dp, (vocab + step) % vocab_count),
            device_id_type=MESH,
        )

    def stats_send(s, ref_side):
        target = my_cots(s)[2]
        peak = jnp.max(peaks[s], axis=1, keepdims=True)
        mass = cross = picked = jnp.zeros((ROWS, LANES), F32)
        for f in range(4):
            values = logits[s, f]
            weights = jnp.exp(values - peak)
            mass = mass + lane_sum(weights)
            cross = cross + lane_sum(weights * (values - ref_piece(s, f)))
            picked = picked + lane_sum(jnp.where(hit(f, target), values, 0.0))
        mass, cross, picked = [
            jnp.sum(value, axis=1, keepdims=True) for value in (mass, cross, picked)
        ]
        packed = jnp.zeros((ROWS, LANES), F32)
        for k, value in enumerate((peak, mass, cross) + ref_side + (picked,)):
            packed = packed + jnp.where(lane == k, value, 0.0)
        stats[s, vocab] = packed
        for step in range(1, vocab_count):
            stats_copy(s, step).start()

    def other_stats(s):
        return stats.at[s, pl.ds(0, vocab_count - 1)]

    def stats_finish(s):
        pltpu.make_async_copy(other_stats(s), other_stats(s), st_recv.at[s]).wait()
        every = [stats[s, k] for k in range(vocab_count)]
        peak, ref_peak = every[0][:, 0:1], every[0][:, 3:4]
        for tile in every[1:]:
            peak = jnp.maximum(peak, tile[:, 0:1])
            ref_peak = jnp.maximum(ref_peak, tile[:, 3:4])
        mass, cross, ref_mass, picked = 0.0, 0.0, 0.0, 0.0
        for tile in every:
            scale = jnp.exp(tile[:, 0:1] - peak)
            mass = mass + tile[:, 1:2] * scale
            cross = cross + tile[:, 2:3] * scale
            ref_mass = ref_mass + tile[:, 4:5] * jnp.exp(tile[:, 3:4] - ref_peak)
            picked = picked + tile[:, 5:6]
        norm = peak + jnp.log(mass)
        ref_norm = ref_peak + jnp.log(ref_mass)
        row_kl = cross / mass - norm + ref_norm
        tokens[here[0], here[1], s * ROWS : (s + 1) * ROWS] = (
            jnp.where(lane == 0, picked - norm, 0.0)
            + jnp.where(lane == 1, row_kl, 0.0)
            + jnp.where(lane == 2, norm, 0.0)
        )
        return norm, ref_norm - norm - row_kl

    half = width // 2

    def gradients(s, norm, shift):
        lp, kl, target = my_cots(s)
        for f in ORDER:
            values = logits[s, f]
            probs = jnp.exp(values - norm)
            excess = values - ref_piece(s, f) + shift
            result = jnp.where(hit(f, target), lp, 0.0) + probs * (kl * excess - lp)
            result = jnp.concatenate([result[:, 0:half], result[:, half:width]], axis=0)
            grads[s, f, here[0], here[1]] = result.astype(BF16)
            for kind in (0, 1, 2):
                ag_copy(s, f, kind).start()

    def relay_copy(buffer, f, kind, straight, send_sem, recv_sem):
        axis, way = FLOWS[f]
        other = 1 - axis
        if kind < 3:
            relayed = kind == 2 and not straight
            spot = place(f, along(axis, -way if relayed else 0), here[other])
            to = device(axis, 2 if kind == 2 and straight else -way if kind == 1 else way)
        else:
            spot = place(f, slice(None), along(other, -way if kind == 5 else 0))
            to = device(other, -way if kind == 4 else way)
        block = buffer.at[spot]
        return pltpu.make_async_remote_copy(
            src_ref=block,
            dst_ref=block,
            send_sem=send_sem,
            recv_sem=recv_sem,
            device_id=to,
            device_id_type=MESH,
        )

    def ag_copy(g, f, kind):
        return relay_copy(
            grads.at[g, f], f, kind, True, ag_send.at[g, kind // 3], ag_recv.at[g, kind, f]
        )

    def ag_pass(g, waits, kinds):
        for f in ORDER:
            for kind in waits:
                ag_copy(g, f, kind).wait_recv()
            for kind in kinds:
                ag_copy(g, f, kind).start()

    def tokens_copy(axis, step):
        block = tokens.at[here] if axis == 1 else tokens.at[here[0]]
        return pltpu.make_async_remote_copy(
            src_ref=block,
            dst_ref=block,
            send_sem=tk_send.at[axis],
            recv_sem=tk_recv.at[axis],
            device_id=device(axis, step),
            device_id_type=MESH,
        )

    def tokens_go(axis):
        for step in range(1, SIDE):
            tokens_copy(axis, step).start()

    def tokens_moved(axis, sem):
        moved = tokens.at[0, pl.ds(0, 3)] if axis == 1 else tokens.at[pl.ds(0, 3)]
        pltpu.make_async_copy(moved, moved, sem.at[axis]).wait()

    def out_copy(g, f):
        return pltpu.make_async_copy(grads.at[g, f], grads_out.at[g, f], out_sem.at[g, f])

    def group_token(g, shape, dim):
        order = iota(shape, dim)
        return (order // ROWS) * rows_dev + g * ROWS + lax.rem(order, ROWS)

    members = count // GROUPS

    def spread(g):
        shape = (count, members)
        chosen = iota(shape, 0) == group_token(g, shape, 1)
        slot_of = jnp.sum(jnp.where(chosen, slot_col.astype(F32), 0.0), axis=0, keepdims=True)
        matches = iota((rows_all, members), 0) == slot_of.astype(I32)
        return jnp.where(matches, 1.0, 0.0).astype(BF16)

    def feature_step(g):
        total = jnp.zeros((members, rows.shape[1]), F32)
        for f in ORDER:
            ag_copy(g, f, 4).wait_recv()
            ag_copy(g, f, 5).wait_recv()
            out_copy(g, f).start()
            for h in range(2):
                piece = grads[g, f, :, :, h * ROWS : (h + 1) * ROWS, :].reshape(members, half)
                total = total + lax.dot_general(
                    piece,
                    weight[f, :, h * half : (h + 1) * half],
                    (((1,), (1,)), ((), ())),
                    preferred_element_type=F32,
                )
        to_slots = spread(g)
        high = total.astype(BF16)
        rest = total - high.astype(F32)
        middle = rest.astype(BF16)
        low = (rest - middle.astype(F32)).astype(BF16)
        placed = jnp.dot(to_slots, high, preferred_element_type=F32)
        placed = placed + jnp.dot(to_slots, middle, preferred_element_type=F32)
        placed = placed + jnp.dot(to_slots, low, preferred_element_type=F32)
        return placed.reshape(slots.shape)

    for f in ORDER:
        multiply(f)
        if f == 0:
            pl.semaphore_wait(barrier, greeted)
        first_ahead(0, f)
        first_back(0, f)
    first_relay(0)
    for f in ORDER:
        first_ahead(1, f)
    for copy in inputs[2:]:
        copy.wait()
    ref32[...] = ref[...].astype(F32)
    lp_col = jnp.sum(jnp.where(placing, cot_lp[...], 0.0), axis=1, keepdims=True)
    kl_col = jnp.sum(jnp.where(placing, cot_kl[...], 0.0), axis=1, keepdims=True)
    target_col = turned(target_row[...].astype(F32))
    lane_all = iota((count, LANES), 1)
    cots[...] = (
        jnp.where(lane_all == 0, lp_col, 0.0)
        + jnp.where(lane_all == 1, kl_col, 0.0)
        + jnp.where(lane_all == 2, target_col, 0.0)
    )
    first_sum(0)
    for f in ORDER:
        first_back(1, f)
    ref_side = [ref_stats(0), ref_stats(1)]
    first_relay(1)
    second_sum(0)
    stats_send(0, ref_side[0])
    first_sum(1)
    gradients(0, *stats_finish(0))
    second_sum(1)
    stats_send(1, ref_side[1])
    ag_pass(0, (0, 1, 2), (3, 4))
    gradients(1, *stats_finish(1))
    ag_pass(0, (3,), (5,))
    ag_pass(1, (0, 1, 2), (3, 4))
    tokens_go(1)
    for g in range(GROUPS):
        rows_turned[:, g * members : (g + 1) * members] = lax.dot_general(
            hidden[...], spread(g), (((0,), (0,)), ((), ())), preferred_element_type=F32
        ).astype(BF16)
    rows_copy = pltpu.make_async_copy(rows_turned, rows_out, end_sem.at[0])
    rows_copy.start()
    ag_pass(1, (3,), (5,))
    tokens_moved(1, tk_recv)
    tokens_go(0)
    slots[...] = feature_step(0)
    slots[...] = slots[...] + feature_step(1)

    core_copy = pltpu.make_async_remote_copy(
        src_ref=slots.at[:, 1 - core],
        dst_ref=core_recv,
        send_sem=core_send_sem,
        recv_sem=core_recv_sem,
        device_id=(dp, level * 2 + 1 - core),
        device_id_type=MESH,
    )
    core_copy.start()

    tokens_moved(0, tk_recv)
    everyone = tokens[...].reshape(count, LANES)
    mine_slots = slot_col == dp * slot_count + lane_all
    mine_slots = mine_slots & (lane_all < slot_count)
    for k in range(3):
        tokens_result[k : k + 1, :] = jnp.sum(
            jnp.where(mine_slots, everyone[:, k : k + 1], 0.0), axis=0, keepdims=True
        )

    tokens_copied = pltpu.make_async_copy(tokens_result, tokens_out, end_sem.at[1])
    tokens_copied.start()
    core_copy.wait_recv()
    slot_rows = slots.shape[2]
    feature_width = slots.shape[3]

    def pair_sum(l):
        return slots[l, core] + core_recv[l]

    def z_copy(step):
        return pltpu.make_async_remote_copy(
            src_ref=zsend.at[step],
            dst_ref=zrecv.at[step],
            send_sem=z_send.at[step],
            recv_sem=z_recv.at[step],
            device_id=(dp, ((level + step) % levels) * 2 + core),
            device_id_type=MESH,
        )

    for step in (2, 1, 3):
        if step < levels:
            both = pair_sum((level + step) % levels)
            encode([both[k : k + ROWS] for k in range(0, slot_rows, ROWS)], zsend.at[step])
            z_copy(step).start()
    total = pair_sum(level)
    for step in range(1, levels):
        z_copy(step).wait_recv()
    pieces_out = []
    for k in range(slot_rows // ROWS):
        block = total[k * ROWS : (k + 1) * ROWS]
        for step in range(1, levels):
            block = block + decode(zrecv.at[step], k, feature_width)
        pieces_out.append(block)
    feature_result[...] = jnp.concatenate(pieces_out, axis=0).astype(BF16)
    feature_copied = pltpu.make_async_copy(feature_result, feature_out, end_sem.at[2])
    feature_copied.start()

    def left(source, sem):
        pltpu.make_async_copy(source, source, sem).wait()

    for s in range(GROUPS):
        left(send1.at[s], rs_send.at[s, 0])
        left(send2.at[s], rs_send.at[s, 1])
    for g in range(GROUPS):
        left(grads.at[g, :, 0, pl.ds(0, 3)], ag_send.at[g, 0])
        left(grads.at[g, pl.ds(0, 3)], ag_send.at[g, 1])
        for f in range(4):
            out_copy(g, f).wait()
        left(other_stats(g), st_send.at[g])
    for axis in range(2):
        tokens_moved(axis, tk_send)
    core_copy.wait_send()
    for step in range(1, levels):
        z_copy(step).wait_send()
    rows_copy.wait()
    tokens_copied.wait()
    feature_copied.wait()


def weight_kernel(
    rows_in,
    grads_in,
    feature_in,
    tokens_in,
    out,
    feature_out,
    first,
    second,
    third,
    rows,
    grads,
    tokens,
    small,
    result,
    in_sem,
    out_sem,
):
    width = grads.shape[5]
    members = rows.shape[1] // GROUPS

    def load(f):
        return pltpu.make_async_copy(grads_in.at[:, f], grads.at[f], in_sem.at[f])

    def store(f, h):
        cols = pl.ds((2 * f + h) * width, width)
        return pltpu.make_async_copy(result.at[f, h], out.at[:, cols], out_sem.at[f, h])

    rows_copy = pltpu.make_async_copy(rows_in, rows, in_sem.at[4])
    rows_copy.start()
    for f in range(4):
        load(f).start()
    tokens_copy = pltpu.make_async_copy(tokens_in, tokens, in_sem.at[5])
    tokens_copy.start()
    feature_copy = pltpu.make_async_copy(feature_in, feature_out, in_sem.at[6])
    feature_copy.start()
    rows_copy.wait()
    for f in range(4):
        load(f).wait()
        for h in range(2):
            block = jnp.concatenate(
                [
                    grads[f, g, :, :, h * ROWS : (h + 1) * ROWS, :].reshape(members, width)
                    for g in range(GROUPS)
                ],
                axis=0,
            )
            result[f, h] = jnp.dot(rows[...], block, preferred_element_type=F32).astype(BF16)
            store(f, h).start()
    tokens_copy.wait()
    outs = []
    for k, token_out in enumerate((first, second, third)):
        small[k] = tokens[k : k + 1, 0 : small.shape[2]]
        outs.append(pltpu.make_async_copy(small.at[k], token_out, in_sem.at[7 + k]))
        outs[-1].start()
    feature_copy.wait()
    for copy in outs:
        copy.wait()
    for f in range(4):
        for h in range(2):
            store(f, h).wait()


def per_device(
    vocab_count, pol_hidden, pol_weight, ref_logits, targets, owners, grad_logprob, grad_kl
):
    all_slots, depth = pol_hidden.shape
    cols = pol_weight.shape[1]
    rows_dev = ref_logits.shape[0]
    count = owners.shape[0]
    chips = SIDE * SIDE
    width = cols // 4
    slot_count = all_slots // chips
    levels = vocab_count // 2
    slot_rows = all_slots // vocab_count
    unit1 = (GROUPS, 4, 3, ROWS, SIDE * width // 2 + LANES)
    unit2 = (GROUPS, 4, 3, ROWS, width // 2 + LANES)
    unit3 = (levels, ROWS, slot_rows // ROWS * depth // 2 + LANES)
    grads_shape = (GROUPS, 4, SIDE, SIDE, rows_dev, width // 2)
    anywhere = pl.BlockSpec(memory_space=pl.ANY)
    flops = 2 * count * depth * cols * 2
    grads, rows, feature, tokens = pl.pallas_call(
        functools.partial(head_kernel, vocab_count),
        out_shape=(
            jax.ShapeDtypeStruct(grads_shape, BF16),
            jax.ShapeDtypeStruct((depth, count), BF16),
            jax.ShapeDtypeStruct((slot_rows, depth), BF16),
            jax.ShapeDtypeStruct((8, LANES), F32),
        ),
        in_specs=[pl.BlockSpec(memory_space=pltpu.HBM)] * 7,
        out_specs=(anywhere,) * 4,
        scratch_shapes=[
            pltpu.VMEM((all_slots, depth), BF16),
            pltpu.VMEM((rows_dev, cols), BF16),
            pltpu.VMEM((1, count), I32),
            pltpu.VMEM((1, count), I32),
            pltpu.VMEM((1, all_slots), F32),
            pltpu.VMEM((1, all_slots), F32),
            pltpu.VMEM((count, depth), BF16),
            pltpu.VMEM((depth, count), BF16),
            pltpu.VMEM((slot_rows, depth), BF16),
            pltpu.VMEM((8, LANES), F32),
            pltpu.VMEM((4, depth, width), BF16),
            pltpu.VMEM((GROUPS, 4, SIDE, SIDE, ROWS, width), F32),
            pltpu.VMEM(unit1, I32),
            pltpu.VMEM(unit1, I32),
            pltpu.VMEM(unit2, I32),
            pltpu.VMEM(unit2, I32),
            pltpu.VMEM((GROUPS, 4, ROWS, width), F32),
            pltpu.VMEM(grads_shape, BF16),
            pltpu.VMEM((GROUPS, ROWS, LANES), F32),
            pltpu.VMEM((count, LANES), F32),
            pltpu.VMEM((GROUPS, vocab_count, ROWS, LANES), F32),
            pltpu.VMEM((SIDE, SIDE, rows_dev, LANES), F32),
            pltpu.VMEM((levels, 2, slot_rows, depth), F32),
            pltpu.VMEM((rows_dev, cols), F32),
            pltpu.VMEM((levels, slot_rows, depth), F32),
            pltpu.VMEM(unit3, I32),
            pltpu.VMEM(unit3, I32),
            pltpu.SemaphoreType.DMA((6,)),
            pltpu.SemaphoreType.DMA((4,)),
            pltpu.SemaphoreType.DMA((GROUPS, 2)),
            pltpu.SemaphoreType.DMA((GROUPS, 6, 4)),
            pltpu.SemaphoreType.DMA((GROUPS, 2)),
            pltpu.SemaphoreType.DMA((GROUPS, 6, 4)),
            pltpu.SemaphoreType.DMA((GROUPS,)),
            pltpu.SemaphoreType.DMA((GROUPS,)),
            pltpu.SemaphoreType.DMA((2,)),
            pltpu.SemaphoreType.DMA((2,)),
            pltpu.SemaphoreType.DMA,
            pltpu.SemaphoreType.DMA,
            pltpu.SemaphoreType.DMA((levels,)),
            pltpu.SemaphoreType.DMA((levels,)),
            pltpu.SemaphoreType.DMA((GROUPS, 4)),
            pltpu.SemaphoreType.DMA((3,)),
        ],
        compiler_params=pltpu.CompilerParams(
            collective_id=0, has_side_effects=True, vmem_limit_bytes=60 * 2**20
        ),
        cost_estimate=pl.CostEstimate(
            flops=flops, bytes_accessed=3 * depth * cols, transcendentals=3 * rows_dev * cols
        ),
        name="head",
    )(
        pol_hidden,
        pol_weight,
        ref_logits,
        targets.reshape(1, count),
        owners.reshape(1, count),
        grad_logprob.reshape(1, all_slots),
        grad_kl.reshape(1, all_slots),
    )
    token_shape = jax.ShapeDtypeStruct((1, slot_count), F32)
    weight_grad, feature, first, second, third = pl.pallas_call(
        weight_kernel,
        out_shape=(
            jax.ShapeDtypeStruct((depth, cols), BF16),
            jax.ShapeDtypeStruct((slot_rows, depth), BF16),
            token_shape,
            token_shape,
            token_shape,
        ),
        in_specs=[anywhere] * 4,
        out_specs=(anywhere,) * 5,
        scratch_shapes=[
            pltpu.VMEM((depth, count), BF16),
            pltpu.VMEM((4, GROUPS) + grads_shape[2:], BF16),
            pltpu.VMEM((8, LANES), F32),
            pltpu.VMEM((3, 1, slot_count), F32),
            pltpu.VMEM((4, 2, depth, width // 2), BF16),
            pltpu.SemaphoreType.DMA((10,)),
            pltpu.SemaphoreType.DMA((4, 2)),
        ],
        compiler_params=pltpu.CompilerParams(vmem_limit_bytes=60 * 2**20),
        cost_estimate=pl.CostEstimate(
            flops=2 * count * depth * cols,
            bytes_accessed=2 * (depth + count) * cols,
            transcendentals=0,
        ),
        name="weight_grad",
    )(rows, grads, feature, tokens)
    return (
        first.reshape(slot_count),
        second.reshape(slot_count),
        third.reshape(slot_count),
        feature,
        weight_grad,
    )


def solution(mesh):
    in_specs = (P(None, "dp"), P("dp", "vocab"), P("dp", "vocab"), P(), P(), P(), P())
    out_specs = (P("dp"), P("dp"), P("dp"), P("vocab", "dp"), P("dp", "vocab"))
    return jax.shard_map(
        functools.partial(per_device, mesh.shape["vocab"]),
        mesh=mesh,
        in_specs=in_specs,
        out_specs=out_specs,
        check_vma=False,
    )
```

```python
import functools

import jax
import jax.numpy as jnp
from jax import lax
from jax.experimental import pallas as pl
from jax.experimental.pallas import tpu as pltpu
from jax.sharding import PartitionSpec as P

F32 = jnp.float32
BF16 = jnp.bfloat16
I32 = jnp.int32
MESH = pl.DeviceIdType.MESH
SIDE = 4
LANES = 128
GROUPS = 2
ROWS = 8
FLOWS = ((0, 1), (0, -1), (1, 1), (1, -1))
ORDER = (0, 2, 1, 3)
LARGEST = 32766.0


def encode(blocks, dst):
    tiles = blocks[0].shape[1] // (2 * LANES)
    parts = []
    for block in blocks:
        for t in range(tiles):
            u = t + tiles
            parts.append(
                (block[:, t * LANES : (t + 1) * LANES], block[:, u * LANES : (u + 1) * LANES])
            )
    peak = jnp.full((ROWS, LANES), 1e-30, F32)
    for high, low in parts:
        peak = jnp.maximum(peak, jnp.maximum(jnp.abs(high), jnp.abs(low)))
    power = jnp.ceil(jnp.log2(peak) * 8.0)
    inverse = jnp.exp2(power * -0.125) * LARGEST
    for k, (high, low) in enumerate(parts):
        high_code = jnp.round(high * inverse).astype(I32)
        low_code = jnp.round(low * inverse).astype(I32)
        dst[:, k * LANES : (k + 1) * LANES] = (high_code << 16) | (low_code & 0xFFFF)
    end = len(parts) * LANES
    dst[:, end : end + LANES] = power.astype(I32)


def decode(src, block, width):
    end = src.shape[1] - LANES
    scale = jnp.exp2(src[:, end : end + LANES].astype(F32) * 0.125) * (1.0 / LARGEST)
    highs, lows = [], []
    for t in range(width // (2 * LANES)):
        start = block * (width // 2) + t * LANES
        word = src[:, start : start + LANES]
        highs.append((word >> 16).astype(F32) * scale)
        lows.append(((word << 16) >> 16).astype(F32) * scale)
    return jnp.concatenate(highs + lows, axis=1)


def head_kernel(
    vocab_count,
    hidden_hbm,
    weight_hbm,
    ref_hbm,
    target_hbm,
    owner_hbm,
    cot_lp_hbm,
    cot_kl_hbm,
    grads_out,
    rows_out,
    feature_out,
    tokens_out,
    hidden,
    ref,
    target_row,
    owner_row,
    cot_lp,
    cot_kl,
    rows,
    rows_turned,
    feature_result,
    tokens_result,
    weight,
    part,
    send1,
    recv1,
    send2,
    recv2,
    logits,
    grads,
    peaks,
    cots,
    stats,
    tokens,
    slots,
    spreads,
    ref32,
    core_recv,
    zsend,
    zrecv,
    in_sem,
    w_sem,
    rs_send,
    rs_recv,
    ag_send,
    ag_recv,
    st_send,
    st_recv,
    tk_send,
    tk_recv,
    core_send_sem,
    core_recv_sem,
    z_send,
    z_recv,
    out_sem,
    end_sem,
):
    width = weight.shape[2]
    rows_all = hidden.shape[0]
    count = owner_row.shape[1]
    chips = SIDE * SIDE
    rows_dev = count // chips
    levels = vocab_count // 2
    dp = lax.axis_index("dp")
    vocab = lax.axis_index("vocab")
    here = (dp // SIDE, dp % SIDE)
    level, core = vocab // 2, vocab % 2

    def along(axis, offset):
        return lax.rem(here[axis] + offset + SIDE, SIDE)

    def device(axis, offset):
        moved = along(axis, offset)
        return (moved * SIDE + here[1], vocab) if axis == 0 else (here[0] * SIDE + moved, vocab)

    def place(f, first, second):
        return (first, second) if FLOWS[f][0] == 0 else (second, first)

    barrier = pltpu.get_barrier_semaphore()
    for axis in range(2):
        for step in range(1, SIDE):
            pl.semaphore_signal(barrier, inc=1, device_id=device(axis, step), device_id_type=MESH)
    for step in range(1, vocab_count):
        pl.semaphore_signal(
            barrier, inc=1, device_id=(dp, (vocab + step) % vocab_count), device_id_type=MESH
        )
    greeted = 2 * (SIDE - 1) + vocab_count - 1

    inputs = [
        pltpu.make_async_copy(source, landing, in_sem.at[k])
        for k, (source, landing) in enumerate(
            (
                (owner_hbm, owner_row),
                (hidden_hbm, hidden),
                (cot_lp_hbm, cot_lp),
                (cot_kl_hbm, cot_kl),
                (target_hbm, target_row),
                (ref_hbm, ref),
            )
        )
    ]
    for copy in inputs:
        copy.start()

    def weight_copy(f):
        cols = pl.ds(f * width, width)
        return pltpu.make_async_copy(weight_hbm.at[:, cols], weight.at[f], w_sem.at[f])

    for f in ORDER:
        weight_copy(f).start()

    def iota(shape, dim):
        return lax.broadcasted_iota(I32, shape, dim)

    inputs[0].wait()
    rows_i, cols_i = iota((count, count), 0), iota((count, count), 1)
    diagonal = rows_i == cols_i

    def turned(row):
        return jnp.sum(jnp.where(diagonal, row, 0), axis=1, keepdims=True)

    owner_col = turned(owner_row[...].astype(F32)).astype(I32)
    alike = (owner_col == owner_row[...]) & (rows_i // rows_dev == cols_i // rows_dev)
    before_col = jnp.sum(jnp.where(alike & (cols_i < rows_i), 1.0, 0.0), axis=1, keepdims=True)
    before_row = jnp.sum(jnp.where(alike & (rows_i < cols_i), 1.0, 0.0), axis=0, keepdims=True)
    slot_count = rows_all // chips
    capacity = slot_count // chips
    slot_col = (
        owner_col * slot_count
        + (iota((count, 1), 0) // rows_dev) * capacity
        + before_col.astype(I32)
    )
    slot_row = (
        owner_row[...] * slot_count
        + (iota((1, count), 1) // rows_dev) * capacity
        + before_row.astype(I32)
    )
    placing = slot_col == iota((count, rows_all), 1)
    inputs[1].wait()
    rows[...] = jnp.dot(
        jnp.where(placing, 1.0, 0.0).astype(BF16), hidden[...], preferred_element_type=F32
    ).astype(BF16)

    def rs_copy(s, f, kind):
        axis, way = FLOWS[f]
        stage, role = kind // 3, kind % 3
        if stage == 1:
            axis = 1 - axis
        source, landing = (send1, recv1) if stage == 0 else (send2, recv2)
        return pltpu.make_async_remote_copy(
            src_ref=source.at[s, f, role],
            dst_ref=landing.at[s, f, role],
            send_sem=rs_send.at[s, stage],
            recv_sem=rs_recv.at[s, kind, f],
            device_id=device(axis, 2 if kind == 3 else -way if role == 1 else way),
            device_id_type=MESH,
        )

    def first_blocks(s, f, offset):
        first = along(FLOWS[f][0], offset)
        return [part[(s, f) + place(f, first, k)] for k in range(SIDE)]

    def second_block(s, f, offset):
        axis = FLOWS[f][0]
        return part[(s, f) + place(f, here[axis], along(1 - axis, offset))]

    def multiply(f):
        weight_copy(f).wait()
        product = jnp.dot(rows[...], weight[f], preferred_element_type=F32)
        product = product.reshape(SIDE, SIDE, rows_dev, width)
        part[0, f] = product[:, :, 0:ROWS]
        part[1, f] = product[:, :, ROWS:rows_dev]

    def first_ahead(s, f):
        encode(first_blocks(s, f, 2), send1.at[s, f, 0])
        rs_copy(s, f, 0).start()

    def first_back(s, f):
        encode(first_blocks(s, f, -FLOWS[f][1]), send1.at[s, f, 1])
        rs_copy(s, f, 1).start()

    def first_relay(s):
        for f in ORDER:
            rs_copy(s, f, 0).wait_recv()
            own = first_blocks(s, f, FLOWS[f][1])
            arrived = recv1.at[s, f, 0]
            encode(
                [own[k] + decode(arrived, k, width) for k in range(SIDE)], send1.at[s, f, 2]
            )
            rs_copy(s, f, 2).start()

    def first_sum(s):
        for f in ORDER:
            rs_copy(s, f, 1).wait_recv()
            rs_copy(s, f, 2).wait_recv()
            axis, way = FLOWS[f]
            for k in range(SIDE):
                spot = (s, f) + place(f, here[axis], k)
                part[spot] = (
                    part[spot]
                    + decode(recv1.at[s, f, 1], k, width)
                    + decode(recv1.at[s, f, 2], k, width)
                )
            for role, offset in ((0, 2), (1, -way), (2, way)):
                encode([second_block(s, f, offset)], send2.at[s, f, role])
                rs_copy(s, f, 3 + role).start()

    def second_sum(s):
        peak = jnp.full((ROWS, LANES), -jnp.inf, F32)
        for f in ORDER:
            for kind in (3, 4, 5):
                rs_copy(s, f, kind).wait_recv()
            done = (
                second_block(s, f, 0)
                + decode(recv2.at[s, f, 0], 0, width)
                + decode(recv2.at[s, f, 1], 0, width)
                + decode(recv2.at[s, f, 2], 0, width)
            )
            logits[s, f] = done
            for t in range(width // LANES):
                peak = jnp.maximum(peak, done[:, t * LANES : (t + 1) * LANES])
        peaks[s] = peak

    def ref_piece(s, f):
        return ref32[s * ROWS : (s + 1) * ROWS, f * width : (f + 1) * width]

    def lane_sum(values):
        total = values[:, 0:LANES]
        for t in range(1, width // LANES):
            total = total + values[:, t * LANES : (t + 1) * LANES]
        return total

    first_col = vocab * (4 * width)
    lane = iota((ROWS, LANES), 1)

    def my_cots(s):
        start = pl.multiple_of(dp * rows_dev, rows_dev) + s * ROWS
        mine = cots[pl.ds(pl.multiple_of(start, ROWS), ROWS), :]
        return mine[:, 0:1], mine[:, 1:2], mine[:, 2:3].astype(I32)

    def hit(f, target):
        return first_col + f * width + iota((ROWS, width), 1) == target

    def ref_stats(s):
        peak = jnp.full((ROWS, 1), -jnp.inf, F32)
        for f in range(4):
            peak = jnp.maximum(peak, jnp.max(ref_piece(s, f), axis=1, keepdims=True))
        mass = jnp.zeros((ROWS, LANES), F32)
        for f in range(4):
            mass = mass + lane_sum(jnp.exp(ref_piece(s, f) - peak))
        return peak, jnp.sum(mass, axis=1, keepdims=True)

    def stats_copy(s, step):
        return pltpu.make_async_remote_copy(
            src_ref=stats.at[s, vocab],
            dst_ref=stats.at[s, vocab],
            send_sem=st_send.at[s],
            recv_sem=st_recv.at[s],
            device_id=(dp, (vocab + step) % vocab_count),
            device_id_type=MESH,
        )

    def stats_send(s, ref_side):
        target = my_cots(s)[2]
        peak = jnp.max(peaks[s], axis=1, keepdims=True)
        mass = cross = picked = jnp.zeros((ROWS, LANES), F32)
        for f in range(4):
            values = logits[s, f]
            weights = jnp.exp(values - peak)
            mass = mass + lane_sum(weights)
            cross = cross + lane_sum(weights * (values - ref_piece(s, f)))
            picked = picked + lane_sum(jnp.where(hit(f, target), values, 0.0))
        mass, cross, picked = [
            jnp.sum(value, axis=1, keepdims=True) for value in (mass, cross, picked)
        ]
        packed = jnp.zeros((ROWS, LANES), F32)
        for k, value in enumerate((peak, mass, cross) + ref_side + (picked,)):
            packed = packed + jnp.where(lane == k, value, 0.0)
        stats[s, vocab] = packed
        for step in range(1, vocab_count):
            stats_copy(s, step).start()

    def other_stats(s):
        return stats.at[s, pl.ds(0, vocab_count - 1)]

    def stats_finish(s):
        pltpu.make_async_copy(other_stats(s), other_stats(s), st_recv.at[s]).wait()
        every = [stats[s, k] for k in range(vocab_count)]
        peak, ref_peak = every[0][:, 0:1], every[0][:, 3:4]
        for tile in every[1:]:
            peak = jnp.maximum(peak, tile[:, 0:1])
            ref_peak = jnp.maximum(ref_peak, tile[:, 3:4])
        mass, cross, ref_mass, picked = 0.0, 0.0, 0.0, 0.0
        for tile in every:
            scale = jnp.exp(tile[:, 0:1] - peak)
            mass = mass + tile[:, 1:2] * scale
            cross = cross + tile[:, 2:3] * scale
            ref_mass = ref_mass + tile[:, 4:5] * jnp.exp(tile[:, 3:4] - ref_peak)
            picked = picked + tile[:, 5:6]
        norm = peak + jnp.log(mass)
        ref_norm = ref_peak + jnp.log(ref_mass)
        row_kl = cross / mass - norm + ref_norm
        tokens[here[0], here[1], s * ROWS : (s + 1) * ROWS] = (
            jnp.where(lane == 0, picked - norm, 0.0)
            + jnp.where(lane == 1, row_kl, 0.0)
            + jnp.where(lane == 2, norm, 0.0)
        )
        return norm, ref_norm - norm - row_kl

    half = width // 2

    def gradients(s, norm, shift):
        lp, kl, target = my_cots(s)
        for f in ORDER:
            values = logits[s, f]
            probs = jnp.exp(values - norm)
            excess = values - ref_piece(s, f) + shift
            result = jnp.where(hit(f, target), lp, 0.0) + probs * (kl * excess - lp)
            result = jnp.concatenate([result[:, 0:half], result[:, half:width]], axis=0)
            grads[s, f, here[0], here[1]] = result.astype(BF16)
            for kind in (0, 1, 2):
                ag_copy(s, f, kind).start()

    def relay_copy(buffer, f, kind, straight, send_sem, recv_sem):
        axis, way = FLOWS[f]
        other = 1 - axis
        if kind < 3:
            relayed = kind == 2 and not straight
            spot = place(f, along(axis, -way if relayed else 0), here[other])
            to = device(axis, 2 if kind == 2 and straight else -way if kind == 1 else way)
        else:
            spot = place(f, slice(None), along(other, -way if kind == 5 else 0))
            to = device(other, -way if kind == 4 else way)
        block = buffer.at[spot]
        return pltpu.make_async_remote_copy(
            src_ref=block,
            dst_ref=block,
            send_sem=send_sem,
            recv_sem=recv_sem,
            device_id=to,
            device_id_type=MESH,
        )

    def ag_copy(g, f, kind):
        return relay_copy(
            grads.at[g, f], f, kind, True, ag_send.at[g, kind // 3], ag_recv.at[g, kind, f]
        )

    def ag_pass(g, waits, kinds):
        for f in ORDER:
            for kind in waits:
                ag_copy(g, f, kind).wait_recv()
            for kind in kinds:
                ag_copy(g, f, kind).start()

    def tokens_copy(axis, step):
        block = tokens.at[here] if axis == 1 else tokens.at[here[0]]
        return pltpu.make_async_remote_copy(
            src_ref=block,
            dst_ref=block,
            send_sem=tk_send.at[axis],
            recv_sem=tk_recv.at[axis],
            device_id=device(axis, step),
            device_id_type=MESH,
        )

    def tokens_go(axis):
        for step in range(1, SIDE):
            tokens_copy(axis, step).start()

    def tokens_moved(axis, sem):
        moved = tokens.at[0, pl.ds(0, 3)] if axis == 1 else tokens.at[pl.ds(0, 3)]
        pltpu.make_async_copy(moved, moved, sem.at[axis]).wait()

    def out_copy(g, f):
        return pltpu.make_async_copy(grads.at[g, f], grads_out.at[g, f], out_sem.at[g, f])

    def group_token(g, shape, dim):
        order = iota(shape, dim)
        return (order // ROWS) * rows_dev + g * ROWS + lax.rem(order, ROWS)

    members = count // GROUPS

    def spread(g):
        shape = (count, members)
        chosen = iota(shape, 0) == group_token(g, shape, 1)
        slot_of = jnp.sum(jnp.where(chosen, slot_col.astype(F32), 0.0), axis=0, keepdims=True)
        matches = iota((rows_all, members), 0) == slot_of.astype(I32)
        return jnp.where(matches, 1.0, 0.0).astype(BF16)

    def feature_step(g):
        total = jnp.zeros((members, rows.shape[1]), F32)
        for f in ORDER:
            ag_copy(g, f, 4).wait_recv()
            ag_copy(g, f, 5).wait_recv()
            out_copy(g, f).start()
            for h in range(2):
                piece = grads[g, f, :, :, h * ROWS : (h + 1) * ROWS, :].reshape(members, half)
                total = total + lax.dot_general(
                    piece,
                    weight[f, :, h * half : (h + 1) * half],
                    (((1,), (1,)), ((), ())),
                    preferred_element_type=F32,
                )
        high = total.astype(BF16)
        rest = total - high.astype(F32)
        middle = rest.astype(BF16)
        low = (rest - middle.astype(F32)).astype(BF16)
        return high, middle, low

    def placed(g, l, split):
        total = 0.0
        for piece in split:
            total = total + jnp.dot(spreads[g, l], piece, preferred_element_type=F32)
        return total.reshape(slots.shape[1:])

    for f in ORDER:
        multiply(f)
        if f == 0:
            pl.semaphore_wait(barrier, greeted)
        first_ahead(0, f)
        first_back(0, f)
    first_relay(0)
    for f in ORDER:
        first_ahead(1, f)
    for copy in inputs[2:]:
        copy.wait()
    ref32[...] = ref[...].astype(F32)
    lp_col = jnp.sum(jnp.where(placing, cot_lp[...], 0.0), axis=1, keepdims=True)
    kl_col = jnp.sum(jnp.where(placing, cot_kl[...], 0.0), axis=1, keepdims=True)
    target_col = turned(target_row[...].astype(F32))
    lane_all = iota((count, LANES), 1)
    cots[...] = (
        jnp.where(lane_all == 0, lp_col, 0.0)
        + jnp.where(lane_all == 1, kl_col, 0.0)
        + jnp.where(lane_all == 2, target_col, 0.0)
    )
    first_sum(0)
    for f in ORDER:
        first_back(1, f)
    ref_side = [ref_stats(0), ref_stats(1)]
    first_relay(1)
    second_sum(0)
    stats_send(0, ref_side[0])
    first_sum(1)
    gradients(0, *stats_finish(0))
    second_sum(1)
    stats_send(1, ref_side[1])
    ag_pass(0, (0, 1, 2), (3, 4))
    gradients(1, *stats_finish(1))
    ag_pass(0, (3,), (5,))
    ag_pass(1, (0, 1, 2), (3, 4))
    tokens_go(1)
    for g in range(GROUPS):
        to_slots = spread(g)
        spreads[g] = to_slots.reshape(spreads.shape[1:])
        rows_turned[:, g * members : (g + 1) * members] = lax.dot_general(
            hidden[...], to_slots, (((0,), (0,)), ((), ())), preferred_element_type=F32
        ).astype(BF16)
    rows_copy = pltpu.make_async_copy(rows_turned, rows_out, end_sem.at[0])
    rows_copy.start()
    ag_pass(1, (3,), (5,))
    tokens_moved(1, tk_recv)
    tokens_go(0)
    split = feature_step(0)
    for l in range(levels):
        slots[l] = placed(0, l, split)

    def core_copy(l):
        return pltpu.make_async_remote_copy(
            src_ref=slots.at[l, 1 - core],
            dst_ref=core_recv.at[l],
            send_sem=core_send_sem.at[l],
            recv_sem=core_recv_sem.at[l],
            device_id=(dp, level * 2 + 1 - core),
            device_id_type=MESH,
        )

    turns = [step for step in (2, 1, 3, 0) if step < levels]
    split = feature_step(1)
    for step in turns:
        l = lax.rem(level + step, levels)
        slots[l] = slots[l] + placed(1, l, split)
        core_copy(l).start()

    slot_rows = slots.shape[2]
    feature_width = slots.shape[3]

    def pair_sum(l):
        core_copy(l).wait_recv()
        return slots[l, core] + core_recv[l]

    def z_copy(step):
        return pltpu.make_async_remote_copy(
            src_ref=zsend.at[step],
            dst_ref=zrecv.at[step],
            send_sem=z_send.at[step],
            recv_sem=z_recv.at[step],
            device_id=(dp, ((level + step) % levels) * 2 + core),
            device_id_type=MESH,
        )

    for step in turns:
        if step > 0:
            both = pair_sum(lax.rem(level + step, levels))
            encode([both[k : k + ROWS] for k in range(0, slot_rows, ROWS)], zsend.at[step])
            z_copy(step).start()
    tokens_moved(0, tk_recv)
    everyone = tokens[...].reshape(count, LANES)
    mine_slots = slot_col == dp * slot_count + lane_all
    mine_slots = mine_slots & (lane_all < slot_count)
    for k in range(3):
        tokens_result[k : k + 1, :] = jnp.sum(
            jnp.where(mine_slots, everyone[:, k : k + 1], 0.0), axis=0, keepdims=True
        )

    tokens_copied = pltpu.make_async_copy(tokens_result, tokens_out, end_sem.at[1])
    tokens_copied.start()
    total = pair_sum(level)
    for step in range(1, levels):
        z_copy(step).wait_recv()
    pieces_out = []
    for k in range(slot_rows // ROWS):
        block = total[k * ROWS : (k + 1) * ROWS]
        for step in range(1, levels):
            block = block + decode(zrecv.at[step], k, feature_width)
        pieces_out.append(block)
    feature_result[...] = jnp.concatenate(pieces_out, axis=0).astype(BF16)
    feature_copied = pltpu.make_async_copy(feature_result, feature_out, end_sem.at[2])
    feature_copied.start()

    def left(source, sem):
        pltpu.make_async_copy(source, source, sem).wait()

    for s in range(GROUPS):
        left(send1.at[s], rs_send.at[s, 0])
        left(send2.at[s], rs_send.at[s, 1])
    for g in range(GROUPS):
        left(grads.at[g, :, 0, pl.ds(0, 3)], ag_send.at[g, 0])
        left(grads.at[g, pl.ds(0, 3)], ag_send.at[g, 1])
        for f in range(4):
            out_copy(g, f).wait()
        left(other_stats(g), st_send.at[g])
    for axis in range(2):
        tokens_moved(axis, tk_send)
    for l in range(levels):
        core_copy(l).wait_send()
    for step in range(1, levels):
        z_copy(step).wait_send()
    rows_copy.wait()
    tokens_copied.wait()
    feature_copied.wait()


def weight_kernel(
    rows_in,
    grads_in,
    feature_in,
    tokens_in,
    out,
    feature_out,
    first,
    second,
    third,
    rows,
    grads,
    tokens,
    small,
    result,
    in_sem,
    out_sem,
):
    width = grads.shape[5]
    members = rows.shape[1] // GROUPS

    def load(f):
        return pltpu.make_async_copy(grads_in.at[:, f], grads.at[f], in_sem.at[f])

    def store(f, h):
        cols = pl.ds((2 * f + h) * width, width)
        return pltpu.make_async_copy(result.at[f, h], out.at[:, cols], out_sem.at[f, h])

    rows_copy = pltpu.make_async_copy(rows_in, rows, in_sem.at[4])
    rows_copy.start()
    for f in range(4):
        load(f).start()
    tokens_copy = pltpu.make_async_copy(tokens_in, tokens, in_sem.at[5])
    tokens_copy.start()
    feature_copy = pltpu.make_async_copy(feature_in, feature_out, in_sem.at[6])
    feature_copy.start()
    rows_copy.wait()
    for f in range(4):
        load(f).wait()
        for h in range(2):
            block = jnp.concatenate(
                [
                    grads[f, g, :, :, h * ROWS : (h + 1) * ROWS, :].reshape(members, width)
                    for g in range(GROUPS)
                ],
                axis=0,
            )
            result[f, h] = jnp.dot(rows[...], block, preferred_element_type=F32).astype(BF16)
            store(f, h).start()
    tokens_copy.wait()
    outs = []
    for k, token_out in enumerate((first, second, third)):
        small[k] = tokens[k : k + 1, 0 : small.shape[2]]
        outs.append(pltpu.make_async_copy(small.at[k], token_out, in_sem.at[7 + k]))
        outs[-1].start()
    feature_copy.wait()
    for copy in outs:
        copy.wait()
    for f in range(4):
        for h in range(2):
            store(f, h).wait()


def per_device(
    vocab_count, pol_hidden, pol_weight, ref_logits, targets, owners, grad_logprob, grad_kl
):
    all_slots, depth = pol_hidden.shape
    cols = pol_weight.shape[1]
    rows_dev = ref_logits.shape[0]
    count = owners.shape[0]
    chips = SIDE * SIDE
    width = cols // 4
    slot_count = all_slots // chips
    levels = vocab_count // 2
    slot_rows = all_slots // vocab_count
    unit1 = (GROUPS, 4, 3, ROWS, SIDE * width // 2 + LANES)
    unit2 = (GROUPS, 4, 3, ROWS, width // 2 + LANES)
    unit3 = (levels, ROWS, slot_rows // ROWS * depth // 2 + LANES)
    grads_shape = (GROUPS, 4, SIDE, SIDE, rows_dev, width // 2)
    anywhere = pl.BlockSpec(memory_space=pl.ANY)
    flops = 2 * count * depth * cols * 2
    grads, rows, feature, tokens = pl.pallas_call(
        functools.partial(head_kernel, vocab_count),
        out_shape=(
            jax.ShapeDtypeStruct(grads_shape, BF16),
            jax.ShapeDtypeStruct((depth, count), BF16),
            jax.ShapeDtypeStruct((slot_rows, depth), BF16),
            jax.ShapeDtypeStruct((8, LANES), F32),
        ),
        in_specs=[pl.BlockSpec(memory_space=pltpu.HBM)] * 7,
        out_specs=(anywhere,) * 4,
        scratch_shapes=[
            pltpu.VMEM((all_slots, depth), BF16),
            pltpu.VMEM((rows_dev, cols), BF16),
            pltpu.VMEM((1, count), I32),
            pltpu.VMEM((1, count), I32),
            pltpu.VMEM((1, all_slots), F32),
            pltpu.VMEM((1, all_slots), F32),
            pltpu.VMEM((count, depth), BF16),
            pltpu.VMEM((depth, count), BF16),
            pltpu.VMEM((slot_rows, depth), BF16),
            pltpu.VMEM((8, LANES), F32),
            pltpu.VMEM((4, depth, width), BF16),
            pltpu.VMEM((GROUPS, 4, SIDE, SIDE, ROWS, width), F32),
            pltpu.VMEM(unit1, I32),
            pltpu.VMEM(unit1, I32),
            pltpu.VMEM(unit2, I32),
            pltpu.VMEM(unit2, I32),
            pltpu.VMEM((GROUPS, 4, ROWS, width), F32),
            pltpu.VMEM(grads_shape, BF16),
            pltpu.VMEM((GROUPS, ROWS, LANES), F32),
            pltpu.VMEM((count, LANES), F32),
            pltpu.VMEM((GROUPS, vocab_count, ROWS, LANES), F32),
            pltpu.VMEM((SIDE, SIDE, rows_dev, LANES), F32),
            pltpu.VMEM((levels, 2, slot_rows, depth), F32),
            pltpu.VMEM((GROUPS, levels, all_slots // levels, count // GROUPS), BF16),
            pltpu.VMEM((rows_dev, cols), F32),
            pltpu.VMEM((levels, slot_rows, depth), F32),
            pltpu.VMEM(unit3, I32),
            pltpu.VMEM(unit3, I32),
            pltpu.SemaphoreType.DMA((6,)),
            pltpu.SemaphoreType.DMA((4,)),
            pltpu.SemaphoreType.DMA((GROUPS, 2)),
            pltpu.SemaphoreType.DMA((GROUPS, 6, 4)),
            pltpu.SemaphoreType.DMA((GROUPS, 2)),
            pltpu.SemaphoreType.DMA((GROUPS, 6, 4)),
            pltpu.SemaphoreType.DMA((GROUPS,)),
            pltpu.SemaphoreType.DMA((GROUPS,)),
            pltpu.SemaphoreType.DMA((2,)),
            pltpu.SemaphoreType.DMA((2,)),
            pltpu.SemaphoreType.DMA((levels,)),
            pltpu.SemaphoreType.DMA((levels,)),
            pltpu.SemaphoreType.DMA((levels,)),
            pltpu.SemaphoreType.DMA((levels,)),
            pltpu.SemaphoreType.DMA((GROUPS, 4)),
            pltpu.SemaphoreType.DMA((3,)),
        ],
        compiler_params=pltpu.CompilerParams(
            collective_id=0, has_side_effects=True, vmem_limit_bytes=60 * 2**20
        ),
        cost_estimate=pl.CostEstimate(
            flops=flops, bytes_accessed=3 * depth * cols, transcendentals=3 * rows_dev * cols
        ),
        name="head",
    )(
        pol_hidden,
        pol_weight,
        ref_logits,
        targets.reshape(1, count),
        owners.reshape(1, count),
        grad_logprob.reshape(1, all_slots),
        grad_kl.reshape(1, all_slots),
    )
    token_shape = jax.ShapeDtypeStruct((1, slot_count), F32)
    weight_grad, feature, first, second, third = pl.pallas_call(
        weight_kernel,
        out_shape=(
            jax.ShapeDtypeStruct((depth, cols), BF16),
            jax.ShapeDtypeStruct((slot_rows, depth), BF16),
            token_shape,
            token_shape,
            token_shape,
        ),
        in_specs=[anywhere] * 4,
        out_specs=(anywhere,) * 5,
        scratch_shapes=[
            pltpu.VMEM((depth, count), BF16),
            pltpu.VMEM((4, GROUPS) + grads_shape[2:], BF16),
            pltpu.VMEM((8, LANES), F32),
            pltpu.VMEM((3, 1, slot_count), F32),
            pltpu.VMEM((4, 2, depth, width // 2), BF16),
            pltpu.SemaphoreType.DMA((10,)),
            pltpu.SemaphoreType.DMA((4, 2)),
        ],
        compiler_params=pltpu.CompilerParams(vmem_limit_bytes=60 * 2**20),
        cost_estimate=pl.CostEstimate(
            flops=2 * count * depth * cols,
            bytes_accessed=2 * (depth + count) * cols,
            transcendentals=0,
        ),
        name="weight_grad",
    )(rows, grads, feature, tokens)
    return (
        first.reshape(slot_count),
        second.reshape(slot_count),
        third.reshape(slot_count),
        feature,
        weight_grad,
    )


def solution(mesh):
    in_specs = (P(None, "dp"), P("dp", "vocab"), P("dp", "vocab"), P(), P(), P(), P())
    out_specs = (P("dp"), P("dp"), P("dp"), P("vocab", "dp"), P("dp", "vocab"))
    return jax.shard_map(
        functools.partial(per_device, mesh.shape["vocab"]),
        mesh=mesh,
        in_specs=in_specs,
        out_specs=out_specs,
        check_vma=False,
    )
```

```python
import functools

import jax
import jax.numpy as jnp
from jax import lax
from jax.experimental import pallas as pl
from jax.experimental.pallas import tpu as pltpu
from jax.sharding import PartitionSpec as P

F32 = jnp.float32
BF16 = jnp.bfloat16
I32 = jnp.int32
MESH = pl.DeviceIdType.MESH
SIDE = 4
LANES = 128
GROUPS = 2
ROWS = 8
FLOWS = ((0, 1), (0, -1), (1, 1), (1, -1))
ORDER = (0, 2, 1, 3)
LARGEST = 32766.0


def encode(blocks, dst):
    tiles = blocks[0].shape[1] // (2 * LANES)
    parts = []
    for block in blocks:
        for t in range(tiles):
            u = t + tiles
            parts.append(
                (block[:, t * LANES : (t + 1) * LANES], block[:, u * LANES : (u + 1) * LANES])
            )
    peak = jnp.full((ROWS, LANES), 1e-30, F32)
    for high, low in parts:
        peak = jnp.maximum(peak, jnp.maximum(jnp.abs(high), jnp.abs(low)))
    power = jnp.ceil(jnp.log2(peak) * 8.0)
    inverse = jnp.exp2(power * -0.125) * LARGEST
    for k, (high, low) in enumerate(parts):
        high_code = jnp.round(high * inverse).astype(I32)
        low_code = jnp.round(low * inverse).astype(I32)
        dst[:, k * LANES : (k + 1) * LANES] = (high_code << 16) | (low_code & 0xFFFF)
    end = len(parts) * LANES
    dst[:, end : end + LANES] = power.astype(I32)


def decode(src, block, width):
    end = src.shape[1] - LANES
    scale = jnp.exp2(src[:, end : end + LANES].astype(F32) * 0.125) * (1.0 / LARGEST)
    highs, lows = [], []
    for t in range(width // (2 * LANES)):
        start = block * (width // 2) + t * LANES
        word = src[:, start : start + LANES]
        highs.append((word >> 16).astype(F32) * scale)
        lows.append(((word << 16) >> 16).astype(F32) * scale)
    return jnp.concatenate(highs + lows, axis=1)


def head_kernel(
    vocab_count,
    hidden_hbm,
    weight_hbm,
    ref_hbm,
    target_hbm,
    owner_hbm,
    cot_lp_hbm,
    cot_kl_hbm,
    grads_out,
    rows_out,
    feature_out,
    tokens_out,
    hidden,
    ref,
    target_row,
    owner_row,
    cot_lp,
    cot_kl,
    rows,
    rows_turned,
    feature_result,
    tokens_result,
    weight,
    part,
    send1,
    recv1,
    send2,
    recv2,
    logits,
    grads,
    peaks,
    cots,
    stats,
    tokens,
    slots,
    spreads,
    ref32,
    core_recv,
    zsend,
    zrecv,
    in_sem,
    w_sem,
    rs_send,
    rs_recv,
    ag_send,
    ag_recv,
    st_send,
    st_recv,
    tk_send,
    tk_recv,
    core_send_sem,
    core_recv_sem,
    z_send,
    z_recv,
    out_sem,
    end_sem,
):
    width = weight.shape[2]
    rows_all = hidden.shape[0]
    count = owner_row.shape[1]
    chips = SIDE * SIDE
    rows_dev = count // chips
    levels = vocab_count // 2
    dp = lax.axis_index("dp")
    vocab = lax.axis_index("vocab")
    here = (dp // SIDE, dp % SIDE)
    level, core = vocab // 2, vocab % 2

    def along(axis, offset):
        return lax.rem(here[axis] + offset + SIDE, SIDE)

    def device(axis, offset):
        moved = along(axis, offset)
        return (moved * SIDE + here[1], vocab) if axis == 0 else (here[0] * SIDE + moved, vocab)

    def place(f, first, second):
        return (first, second) if FLOWS[f][0] == 0 else (second, first)

    barrier = pltpu.get_barrier_semaphore()
    for axis in range(2):
        for step in range(1, SIDE):
            pl.semaphore_signal(barrier, inc=1, device_id=device(axis, step), device_id_type=MESH)
    for step in range(1, vocab_count):
        pl.semaphore_signal(
            barrier, inc=1, device_id=(dp, (vocab + step) % vocab_count), device_id_type=MESH
        )
    greeted = 2 * (SIDE - 1) + vocab_count - 1

    inputs = [
        pltpu.make_async_copy(source, landing, in_sem.at[k])
        for k, (source, landing) in enumerate(
            (
                (owner_hbm, owner_row),
                (hidden_hbm, hidden),
                (cot_lp_hbm, cot_lp),
                (cot_kl_hbm, cot_kl),
                (target_hbm, target_row),
                (ref_hbm, ref),
            )
        )
    ]
    for copy in inputs:
        copy.start()

    def weight_copy(f):
        cols = pl.ds(f * width, width)
        return pltpu.make_async_copy(weight_hbm.at[:, cols], weight.at[f], w_sem.at[f])

    for f in ORDER:
        weight_copy(f).start()

    def iota(shape, dim):
        return lax.broadcasted_iota(I32, shape, dim)

    inputs[0].wait()
    rows_i, cols_i = iota((count, count), 0), iota((count, count), 1)
    diagonal = rows_i == cols_i

    def turned(row):
        return jnp.sum(jnp.where(diagonal, row, 0), axis=1, keepdims=True)

    owner_col = turned(owner_row[...].astype(F32)).astype(I32)
    alike = (owner_col == owner_row[...]) & (rows_i // rows_dev == cols_i // rows_dev)
    before_col = jnp.sum(jnp.where(alike & (cols_i < rows_i), 1.0, 0.0), axis=1, keepdims=True)
    before_row = jnp.sum(jnp.where(alike & (rows_i < cols_i), 1.0, 0.0), axis=0, keepdims=True)
    slot_count = rows_all // chips
    capacity = slot_count // chips
    slot_col = (
        owner_col * slot_count
        + (iota((count, 1), 0) // rows_dev) * capacity
        + before_col.astype(I32)
    )
    slot_row = (
        owner_row[...] * slot_count
        + (iota((1, count), 1) // rows_dev) * capacity
        + before_row.astype(I32)
    )
    placing = slot_col == iota((count, rows_all), 1)
    inputs[1].wait()
    rows[...] = jnp.dot(
        jnp.where(placing, 1.0, 0.0).astype(BF16), hidden[...], preferred_element_type=F32
    ).astype(BF16)

    def rs_copy(s, f, kind):
        axis, way = FLOWS[f]
        stage, role = kind // 3, kind % 3
        if stage == 1:
            axis = 1 - axis
        source, landing = (send1, recv1) if stage == 0 else (send2, recv2)
        return pltpu.make_async_remote_copy(
            src_ref=source.at[s, f, role],
            dst_ref=landing.at[s, f, role],
            send_sem=rs_send.at[s, stage],
            recv_sem=rs_recv.at[s, kind, f],
            device_id=device(axis, 2 if kind == 3 else -way if role == 1 else way),
            device_id_type=MESH,
        )

    def first_blocks(s, f, offset):
        first = along(FLOWS[f][0], offset)
        return [part[(s, f) + place(f, first, k)] for k in range(SIDE)]

    def second_block(s, f, offset):
        axis = FLOWS[f][0]
        return part[(s, f) + place(f, here[axis], along(1 - axis, offset))]

    def multiply(f):
        weight_copy(f).wait()
        product = jnp.dot(rows[...], weight[f], preferred_element_type=F32)
        product = product.reshape(SIDE, SIDE, rows_dev, width)
        part[0, f] = product[:, :, 0:ROWS]
        part[1, f] = product[:, :, ROWS:rows_dev]

    def first_ahead(s, f):
        encode(first_blocks(s, f, 2), send1.at[s, f, 0])
        rs_copy(s, f, 0).start()

    def first_back(s, f):
        encode(first_blocks(s, f, -FLOWS[f][1]), send1.at[s, f, 1])
        rs_copy(s, f, 1).start()

    def first_relay(s):
        for f in ORDER:
            rs_copy(s, f, 0).wait_recv()
            own = first_blocks(s, f, FLOWS[f][1])
            arrived = recv1.at[s, f, 0]
            encode(
                [own[k] + decode(arrived, k, width) for k in range(SIDE)], send1.at[s, f, 2]
            )
            rs_copy(s, f, 2).start()

    def first_sum(s):
        for f in ORDER:
            rs_copy(s, f, 1).wait_recv()
            rs_copy(s, f, 2).wait_recv()
            axis, way = FLOWS[f]
            for k in range(SIDE):
                spot = (s, f) + place(f, here[axis], k)
                part[spot] = (
                    part[spot]
                    + decode(recv1.at[s, f, 1], k, width)
                    + decode(recv1.at[s, f, 2], k, width)
                )
            for role, offset in ((0, 2), (1, -way), (2, way)):
                encode([second_block(s, f, offset)], send2.at[s, f, role])
                rs_copy(s, f, 3 + role).start()

    def second_sum(s):
        peak = jnp.full((ROWS, LANES), -jnp.inf, F32)
        for f in ORDER:
            for kind in (3, 4, 5):
                rs_copy(s, f, kind).wait_recv()
            done = (
                second_block(s, f, 0)
                + decode(recv2.at[s, f, 0], 0, width)
                + decode(recv2.at[s, f, 1], 0, width)
                + decode(recv2.at[s, f, 2], 0, width)
            )
            logits[s, f] = done
            for t in range(width // LANES):
                peak = jnp.maximum(peak, done[:, t * LANES : (t + 1) * LANES])
        peaks[s] = peak

    def ref_piece(s, f):
        return ref32[s * ROWS : (s + 1) * ROWS, f * width : (f + 1) * width]

    def lane_sum(values):
        total = values[:, 0:LANES]
        for t in range(1, width // LANES):
            total = total + values[:, t * LANES : (t + 1) * LANES]
        return total

    first_col = vocab * (4 * width)
    lane = iota((ROWS, LANES), 1)

    def my_cots(s):
        start = pl.multiple_of(dp * rows_dev, rows_dev) + s * ROWS
        mine = cots[pl.ds(pl.multiple_of(start, ROWS), ROWS), :]
        return mine[:, 0:1], mine[:, 1:2], mine[:, 2:3].astype(I32)

    def hit(f, target):
        return first_col + f * width + iota((ROWS, width), 1) == target

    def ref_stats(s):
        peak = jnp.full((ROWS, 1), -jnp.inf, F32)
        for f in range(4):
            peak = jnp.maximum(peak, jnp.max(ref_piece(s, f), axis=1, keepdims=True))
        mass = jnp.zeros((ROWS, LANES), F32)
        for f in range(4):
            mass = mass + lane_sum(jnp.exp(ref_piece(s, f) - peak))
        return peak, jnp.sum(mass, axis=1, keepdims=True)

    def stats_copy(s, step):
        return pltpu.make_async_remote_copy(
            src_ref=stats.at[s, vocab],
            dst_ref=stats.at[s, vocab],
            send_sem=st_send.at[s],
            recv_sem=st_recv.at[s],
            device_id=(dp, (vocab + step) % vocab_count),
            device_id_type=MESH,
        )

    def stats_send(s, ref_side):
        target = my_cots(s)[2]
        peak = jnp.max(peaks[s], axis=1, keepdims=True)
        mass = cross = picked = jnp.zeros((ROWS, LANES), F32)
        for f in range(4):
            values = logits[s, f]
            weights = jnp.exp(values - peak)
            mass = mass + lane_sum(weights)
            cross = cross + lane_sum(weights * (values - ref_piece(s, f)))
            picked = picked + lane_sum(jnp.where(hit(f, target), values, 0.0))
        mass, cross, picked = [
            jnp.sum(value, axis=1, keepdims=True) for value in (mass, cross, picked)
        ]
        packed = jnp.zeros((ROWS, LANES), F32)
        for k, value in enumerate((peak, mass, cross) + ref_side + (picked,)):
            packed = packed + jnp.where(lane == k, value, 0.0)
        stats[s, vocab] = packed
        for step in range(1, vocab_count):
            stats_copy(s, step).start()

    def other_stats(s):
        return stats.at[s, pl.ds(0, vocab_count - 1)]

    def stats_finish(s):
        pltpu.make_async_copy(other_stats(s), other_stats(s), st_recv.at[s]).wait()
        every = [stats[s, k] for k in range(vocab_count)]
        peak, ref_peak = every[0][:, 0:1], every[0][:, 3:4]
        for tile in every[1:]:
            peak = jnp.maximum(peak, tile[:, 0:1])
            ref_peak = jnp.maximum(ref_peak, tile[:, 3:4])
        mass, cross, ref_mass, picked = 0.0, 0.0, 0.0, 0.0
        for tile in every:
            scale = jnp.exp(tile[:, 0:1] - peak)
            mass = mass + tile[:, 1:2] * scale
            cross = cross + tile[:, 2:3] * scale
            ref_mass = ref_mass + tile[:, 4:5] * jnp.exp(tile[:, 3:4] - ref_peak)
            picked = picked + tile[:, 5:6]
        norm = peak + jnp.log(mass)
        ref_norm = ref_peak + jnp.log(ref_mass)
        row_kl = cross / mass - norm + ref_norm
        tokens[here[0], here[1], s * ROWS : (s + 1) * ROWS] = (
            jnp.where(lane == 0, picked - norm, 0.0)
            + jnp.where(lane == 1, row_kl, 0.0)
            + jnp.where(lane == 2, norm, 0.0)
        )
        return norm, ref_norm - norm - row_kl

    half = width // 2

    def gradients(s, norm, shift):
        lp, kl, target = my_cots(s)
        for f in ORDER:
            values = logits[s, f]
            probs = jnp.exp(values - norm)
            excess = values - ref_piece(s, f) + shift
            result = jnp.where(hit(f, target), lp, 0.0) + probs * (kl * excess - lp)
            result = jnp.concatenate([result[:, 0:half], result[:, half:width]], axis=0)
            grads[s, f, here[0], here[1]] = result.astype(BF16)
            for kind in (0, 1, 2):
                ag_copy(s, f, kind).start()
            if s == 0:
                line_go(f, 0)

    def relay_copy(buffer, f, kind, straight, send_sem, recv_sem):
        axis, way = FLOWS[f]
        other = 1 - axis
        if kind < 3:
            relayed = kind == 2 and not straight
            spot = place(f, along(axis, -way if relayed else 0), here[other])
            to = device(axis, 2 if kind == 2 and straight else -way if kind == 1 else way)
        else:
            spot = place(f, slice(None), along(other, -way if kind == 5 else 0))
            to = device(other, -way if kind == 4 else way)
        block = buffer.at[spot]
        return pltpu.make_async_remote_copy(
            src_ref=block,
            dst_ref=block,
            send_sem=send_sem,
            recv_sem=recv_sem,
            device_id=to,
            device_id_type=MESH,
        )

    def ag_copy(g, f, kind):
        return relay_copy(
            grads.at[g, f], f, kind, True, ag_send.at[g, kind // 3], ag_recv.at[g, kind, f]
        )

    def line_go(f, offset):
        axis, way = FLOWS[f]
        block = grads.at[(0, f) + place(f, along(axis, offset), here[1 - axis])]
        for kind, to in ((3, way), (4, -way)):
            pltpu.make_async_remote_copy(
                src_ref=block,
                dst_ref=block,
                send_sem=ag_send.at[0, 1],
                recv_sem=ag_recv.at[0, kind, f],
                device_id=device(1 - axis, to),
                device_id_type=MESH,
            ).start()

    def ag_pass(g, waits, kinds):
        for f in ORDER:
            for kind in waits:
                ag_copy(g, f, kind).wait_recv()
            for kind in kinds:
                ag_copy(g, f, kind).start()

    def tokens_copy(axis, step):
        block = tokens.at[here] if axis == 1 else tokens.at[here[0]]
        return pltpu.make_async_remote_copy(
            src_ref=block,
            dst_ref=block,
            send_sem=tk_send.at[axis],
            recv_sem=tk_recv.at[axis],
            device_id=device(axis, step),
            device_id_type=MESH,
        )

    def tokens_go(axis):
        for step in range(1, SIDE):
            tokens_copy(axis, step).start()

    def tokens_moved(axis, sem):
        moved = tokens.at[0, pl.ds(0, 3)] if axis == 1 else tokens.at[pl.ds(0, 3)]
        pltpu.make_async_copy(moved, moved, sem.at[axis]).wait()

    def out_copy(g, f):
        return pltpu.make_async_copy(grads.at[g, f], grads_out.at[g, f], out_sem.at[g, f])

    def group_token(g, shape, dim):
        order = iota(shape, dim)
        return (order // ROWS) * rows_dev + g * ROWS + lax.rem(order, ROWS)

    members = count // GROUPS

    def spread(g):
        shape = (count, members)
        chosen = iota(shape, 0) == group_token(g, shape, 1)
        slot_of = jnp.sum(jnp.where(chosen, slot_col.astype(F32), 0.0), axis=0, keepdims=True)
        matches = iota((rows_all, members), 0) == slot_of.astype(I32)
        return jnp.where(matches, 1.0, 0.0).astype(BF16)

    def feature_step(g):
        total = jnp.zeros((members, rows.shape[1]), F32)
        for f in ORDER:
            ag_copy(g, f, 4).wait_recv()
            ag_copy(g, f, 5).wait_recv()
            out_copy(g, f).start()
            for h in range(2):
                piece = grads[g, f, :, :, h * ROWS : (h + 1) * ROWS, :].reshape(members, half)
                total = total + lax.dot_general(
                    piece,
                    weight[f, :, h * half : (h + 1) * half],
                    (((1,), (1,)), ((), ())),
                    preferred_element_type=F32,
                )
        high = total.astype(BF16)
        rest = total - high.astype(F32)
        middle = rest.astype(BF16)
        low = (rest - middle.astype(F32)).astype(BF16)
        return high, middle, low

    def placed(g, l, split):
        total = 0.0
        for piece in split:
            total = total + jnp.dot(spreads[g, l], piece, preferred_element_type=F32)
        return total.reshape(slots.shape[1:])

    for f in ORDER:
        multiply(f)
        if f == 0:
            pl.semaphore_wait(barrier, greeted)
        first_ahead(0, f)
        first_back(0, f)
    first_relay(0)
    for f in ORDER:
        first_ahead(1, f)
    for copy in inputs[2:]:
        copy.wait()
    ref32[...] = ref[...].astype(F32)
    lp_col = jnp.sum(jnp.where(placing, cot_lp[...], 0.0), axis=1, keepdims=True)
    kl_col = jnp.sum(jnp.where(placing, cot_kl[...], 0.0), axis=1, keepdims=True)
    target_col = turned(target_row[...].astype(F32))
    lane_all = iota((count, LANES), 1)
    cots[...] = (
        jnp.where(lane_all == 0, lp_col, 0.0)
        + jnp.where(lane_all == 1, kl_col, 0.0)
        + jnp.where(lane_all == 2, target_col, 0.0)
    )
    first_sum(0)
    for f in ORDER:
        first_back(1, f)
    ref_side = [ref_stats(0), ref_stats(1)]
    first_relay(1)
    second_sum(0)
    stats_send(0, ref_side[0])
    first_sum(1)
    gradients(0, *stats_finish(0))
    second_sum(1)
    stats_send(1, ref_side[1])
    for kind in (0, 1, 2):
        for f in ORDER:
            ag_copy(0, f, kind).wait_recv()
            line_go(f, (-FLOWS[f][1], FLOWS[f][1], 2)[kind])
    gradients(1, *stats_finish(1))
    ag_pass(0, (3,), (5,))
    ag_pass(1, (0, 1, 2), (3, 4))
    tokens_go(1)
    for g in range(GROUPS):
        to_slots = spread(g)
        spreads[g] = to_slots.reshape(spreads.shape[1:])
        rows_turned[:, g * members : (g + 1) * members] = lax.dot_general(
            hidden[...], to_slots, (((0,), (0,)), ((), ())), preferred_element_type=F32
        ).astype(BF16)
    rows_copy = pltpu.make_async_copy(rows_turned, rows_out, end_sem.at[0])
    rows_copy.start()
    ag_pass(1, (3,), (5,))
    tokens_moved(1, tk_recv)
    tokens_go(0)
    split = feature_step(0)
    for l in range(levels):
        slots[l] = placed(0, l, split)

    def core_copy(l):
        return pltpu.make_async_remote_copy(
            src_ref=slots.at[l, 1 - core],
            dst_ref=core_recv.at[l],
            send_sem=core_send_sem.at[l],
            recv_sem=core_recv_sem.at[l],
            device_id=(dp, level * 2 + 1 - core),
            device_id_type=MESH,
        )

    turns = [step for step in (2, 1, 3, 0) if step < levels]
    split = feature_step(1)
    for step in turns:
        l = lax.rem(level + step, levels)
        slots[l] = slots[l] + placed(1, l, split)
        core_copy(l).start()

    slot_rows = slots.shape[2]
    feature_width = slots.shape[3]

    def pair_sum(l):
        core_copy(l).wait_recv()
        return slots[l, core] + core_recv[l]

    def z_copy(step):
        return pltpu.make_async_remote_copy(
            src_ref=zsend.at[step],
            dst_ref=zrecv.at[step],
            send_sem=z_send.at[step],
            recv_sem=z_recv.at[step],
            device_id=(dp, ((level + step) % levels) * 2 + core),
            device_id_type=MESH,
        )

    for step in turns:
        if step > 0:
            both = pair_sum(lax.rem(level + step, levels))
            encode([both[k : k + ROWS] for k in range(0, slot_rows, ROWS)], zsend.at[step])
            z_copy(step).start()
    tokens_moved(0, tk_recv)
    everyone = tokens[...].reshape(count, LANES)
    mine_slots = slot_col == dp * slot_count + lane_all
    mine_slots = mine_slots & (lane_all < slot_count)
    for k in range(3):
        tokens_result[k : k + 1, :] = jnp.sum(
            jnp.where(mine_slots, everyone[:, k : k + 1], 0.0), axis=0, keepdims=True
        )

    tokens_copied = pltpu.make_async_copy(tokens_result, tokens_out, end_sem.at[1])
    tokens_copied.start()
    total = pair_sum(level)
    for step in range(1, levels):
        z_copy(step).wait_recv()
    pieces_out = []
    for k in range(slot_rows // ROWS):
        block = total[k * ROWS : (k + 1) * ROWS]
        for step in range(1, levels):
            block = block + decode(zrecv.at[step], k, feature_width)
        pieces_out.append(block)
    feature_result[...] = jnp.concatenate(pieces_out, axis=0).astype(BF16)
    feature_copied = pltpu.make_async_copy(feature_result, feature_out, end_sem.at[2])
    feature_copied.start()

    def left(source, sem):
        pltpu.make_async_copy(source, source, sem).wait()

    for s in range(GROUPS):
        left(send1.at[s], rs_send.at[s, 0])
        left(send2.at[s], rs_send.at[s, 1])
    for g in range(GROUPS):
        left(grads.at[g, :, 0, pl.ds(0, 3)], ag_send.at[g, 0])
        left(grads.at[g, pl.ds(0, 3)], ag_send.at[g, 1])
        for f in range(4):
            out_copy(g, f).wait()
        left(other_stats(g), st_send.at[g])
    for axis in range(2):
        tokens_moved(axis, tk_send)
    for l in range(levels):
        core_copy(l).wait_send()
    for step in range(1, levels):
        z_copy(step).wait_send()
    rows_copy.wait()
    tokens_copied.wait()
    feature_copied.wait()


def weight_kernel(
    rows_in,
    grads_in,
    feature_in,
    tokens_in,
    out,
    feature_out,
    first,
    second,
    third,
    rows,
    grads,
    tokens,
    small,
    result,
    in_sem,
    out_sem,
):
    width = grads.shape[5]
    members = rows.shape[1] // GROUPS

    def load(f):
        return pltpu.make_async_copy(grads_in.at[:, f], grads.at[f], in_sem.at[f])

    def store(f, h):
        cols = pl.ds((2 * f + h) * width, width)
        return pltpu.make_async_copy(result.at[f, h], out.at[:, cols], out_sem.at[f, h])

    rows_copy = pltpu.make_async_copy(rows_in, rows, in_sem.at[4])
    rows_copy.start()
    for f in range(4):
        load(f).start()
    tokens_copy = pltpu.make_async_copy(tokens_in, tokens, in_sem.at[5])
    tokens_copy.start()
    feature_copy = pltpu.make_async_copy(feature_in, feature_out, in_sem.at[6])
    feature_copy.start()
    rows_copy.wait()
    for f in range(4):
        load(f).wait()
        for h in range(2):
            block = jnp.concatenate(
                [
                    grads[f, g, :, :, h * ROWS : (h + 1) * ROWS, :].reshape(members, width)
                    for g in range(GROUPS)
                ],
                axis=0,
            )
            result[f, h] = jnp.dot(rows[...], block, preferred_element_type=F32).astype(BF16)
            store(f, h).start()
    tokens_copy.wait()
    outs = []
    for k, token_out in enumerate((first, second, third)):
        small[k] = tokens[k : k + 1, 0 : small.shape[2]]
        outs.append(pltpu.make_async_copy(small.at[k], token_out, in_sem.at[7 + k]))
        outs[-1].start()
    feature_copy.wait()
    for copy in outs:
        copy.wait()
    for f in range(4):
        for h in range(2):
            store(f, h).wait()


def per_device(
    vocab_count, pol_hidden, pol_weight, ref_logits, targets, owners, grad_logprob, grad_kl
):
    all_slots, depth = pol_hidden.shape
    cols = pol_weight.shape[1]
    rows_dev = ref_logits.shape[0]
    count = owners.shape[0]
    chips = SIDE * SIDE
    width = cols // 4
    slot_count = all_slots // chips
    levels = vocab_count // 2
    slot_rows = all_slots // vocab_count
    unit1 = (GROUPS, 4, 3, ROWS, SIDE * width // 2 + LANES)
    unit2 = (GROUPS, 4, 3, ROWS, width // 2 + LANES)
    unit3 = (levels, ROWS, slot_rows // ROWS * depth // 2 + LANES)
    grads_shape = (GROUPS, 4, SIDE, SIDE, rows_dev, width // 2)
    anywhere = pl.BlockSpec(memory_space=pl.ANY)
    flops = 2 * count * depth * cols * 2
    grads, rows, feature, tokens = pl.pallas_call(
        functools.partial(head_kernel, vocab_count),
        out_shape=(
            jax.ShapeDtypeStruct(grads_shape, BF16),
            jax.ShapeDtypeStruct((depth, count), BF16),
            jax.ShapeDtypeStruct((slot_rows, depth), BF16),
            jax.ShapeDtypeStruct((8, LANES), F32),
        ),
        in_specs=[pl.BlockSpec(memory_space=pltpu.HBM)] * 7,
        out_specs=(anywhere,) * 4,
        scratch_shapes=[
            pltpu.VMEM((all_slots, depth), BF16),
            pltpu.VMEM((rows_dev, cols), BF16),
            pltpu.VMEM((1, count), I32),
            pltpu.VMEM((1, count), I32),
            pltpu.VMEM((1, all_slots), F32),
            pltpu.VMEM((1, all_slots), F32),
            pltpu.VMEM((count, depth), BF16),
            pltpu.VMEM((depth, count), BF16),
            pltpu.VMEM((slot_rows, depth), BF16),
            pltpu.VMEM((8, LANES), F32),
            pltpu.VMEM((4, depth, width), BF16),
            pltpu.VMEM((GROUPS, 4, SIDE, SIDE, ROWS, width), F32),
            pltpu.VMEM(unit1, I32),
            pltpu.VMEM(unit1, I32),
            pltpu.VMEM(unit2, I32),
            pltpu.VMEM(unit2, I32),
            pltpu.VMEM((GROUPS, 4, ROWS, width), F32),
            pltpu.VMEM(grads_shape, BF16),
            pltpu.VMEM((GROUPS, ROWS, LANES), F32),
            pltpu.VMEM((count, LANES), F32),
            pltpu.VMEM((GROUPS, vocab_count, ROWS, LANES), F32),
            pltpu.VMEM((SIDE, SIDE, rows_dev, LANES), F32),
            pltpu.VMEM((levels, 2, slot_rows, depth), F32),
            pltpu.VMEM((GROUPS, levels, all_slots // levels, count // GROUPS), BF16),
            pltpu.VMEM((rows_dev, cols), F32),
            pltpu.VMEM((levels, slot_rows, depth), F32),
            pltpu.VMEM(unit3, I32),
            pltpu.VMEM(unit3, I32),
            pltpu.SemaphoreType.DMA((6,)),
            pltpu.SemaphoreType.DMA((4,)),
            pltpu.SemaphoreType.DMA((GROUPS, 2)),
            pltpu.SemaphoreType.DMA((GROUPS, 6, 4)),
            pltpu.SemaphoreType.DMA((GROUPS, 2)),
            pltpu.SemaphoreType.DMA((GROUPS, 6, 4)),
            pltpu.SemaphoreType.DMA((GROUPS,)),
            pltpu.SemaphoreType.DMA((GROUPS,)),
            pltpu.SemaphoreType.DMA((2,)),
            pltpu.SemaphoreType.DMA((2,)),
            pltpu.SemaphoreType.DMA((levels,)),
            pltpu.SemaphoreType.DMA((levels,)),
            pltpu.SemaphoreType.DMA((levels,)),
            pltpu.SemaphoreType.DMA((levels,)),
            pltpu.SemaphoreType.DMA((GROUPS, 4)),
            pltpu.SemaphoreType.DMA((3,)),
        ],
        compiler_params=pltpu.CompilerParams(
            collective_id=0, has_side_effects=True, vmem_limit_bytes=60 * 2**20
        ),
        cost_estimate=pl.CostEstimate(
            flops=flops, bytes_accessed=3 * depth * cols, transcendentals=3 * rows_dev * cols
        ),
        name="head",
    )(
        pol_hidden,
        pol_weight,
        ref_logits,
        targets.reshape(1, count),
        owners.reshape(1, count),
        grad_logprob.reshape(1, all_slots),
        grad_kl.reshape(1, all_slots),
    )
    token_shape = jax.ShapeDtypeStruct((1, slot_count), F32)
    weight_grad, feature, first, second, third = pl.pallas_call(
        weight_kernel,
        out_shape=(
            jax.ShapeDtypeStruct((depth, cols), BF16),
            jax.ShapeDtypeStruct((slot_rows, depth), BF16),
            token_shape,
            token_shape,
            token_shape,
        ),
        in_specs=[anywhere] * 4,
        out_specs=(anywhere,) * 5,
        scratch_shapes=[
            pltpu.VMEM((depth, count), BF16),
            pltpu.VMEM((4, GROUPS) + grads_shape[2:], BF16),
            pltpu.VMEM((8, LANES), F32),
            pltpu.VMEM((3, 1, slot_count), F32),
            pltpu.VMEM((4, 2, depth, width // 2), BF16),
            pltpu.SemaphoreType.DMA((10,)),
            pltpu.SemaphoreType.DMA((4, 2)),
        ],
        compiler_params=pltpu.CompilerParams(vmem_limit_bytes=60 * 2**20),
        cost_estimate=pl.CostEstimate(
            flops=2 * count * depth * cols,
            bytes_accessed=2 * (depth + count) * cols,
            transcendentals=0,
        ),
        name="weight_grad",
    )(rows, grads, feature, tokens)
    return (
        first.reshape(slot_count),
        second.reshape(slot_count),
        third.reshape(slot_count),
        feature,
        weight_grad,
    )


def solution(mesh):
    in_specs = (P(None, "dp"), P("dp", "vocab"), P("dp", "vocab"), P(), P(), P(), P())
    out_specs = (P("dp"), P("dp"), P("dp"), P("vocab", "dp"), P("dp", "vocab"))
    return jax.shard_map(
        functools.partial(per_device, mesh.shape["vocab"]),
        mesh=mesh,
        in_specs=in_specs,
        out_specs=out_specs,
        check_vma=False,
    )
```

```python
import functools

import jax
import jax.numpy as jnp
from jax import lax
from jax.experimental import pallas as pl
from jax.experimental.pallas import tpu as pltpu
from jax.sharding import PartitionSpec as P

F32 = jnp.float32
BF16 = jnp.bfloat16
I32 = jnp.int32
MESH = pl.DeviceIdType.MESH
SIDE = 4
LANES = 128
GROUPS = 2
ROWS = 8
FLOWS = ((0, 1), (0, -1), (1, 1), (1, -1))
ORDER = (0, 2, 1, 3)
LARGEST = 32766.0


def encode(blocks, dst):
    tiles = blocks[0].shape[1] // (2 * LANES)
    parts = []
    for block in blocks:
        for t in range(tiles):
            u = t + tiles
            parts.append(
                (block[:, t * LANES : (t + 1) * LANES], block[:, u * LANES : (u + 1) * LANES])
            )
    peak = jnp.full((ROWS, LANES), 1e-30, F32)
    for high, low in parts:
        peak = jnp.maximum(peak, jnp.maximum(jnp.abs(high), jnp.abs(low)))
    power = jnp.ceil(jnp.log2(peak) * 8.0)
    inverse = jnp.exp2(power * -0.125) * LARGEST
    for k, (high, low) in enumerate(parts):
        high_code = jnp.round(high * inverse).astype(I32)
        low_code = jnp.round(low * inverse).astype(I32)
        dst[:, k * LANES : (k + 1) * LANES] = (high_code << 16) | (low_code & 0xFFFF)
    end = len(parts) * LANES
    dst[:, end : end + LANES] = power.astype(I32)


def decode(src, block, width):
    end = src.shape[1] - LANES
    scale = jnp.exp2(src[:, end : end + LANES].astype(F32) * 0.125) * (1.0 / LARGEST)
    highs, lows = [], []
    for t in range(width // (2 * LANES)):
        start = block * (width // 2) + t * LANES
        word = src[:, start : start + LANES]
        highs.append((word >> 16).astype(F32) * scale)
        lows.append(((word << 16) >> 16).astype(F32) * scale)
    return jnp.concatenate(highs + lows, axis=1)


def head_kernel(
    vocab_count,
    hidden_hbm,
    weight_hbm,
    ref_hbm,
    target_hbm,
    owner_hbm,
    cot_lp_hbm,
    cot_kl_hbm,
    grads_out,
    rows_out,
    feature_out,
    tokens_out,
    hidden,
    ref,
    target_row,
    owner_row,
    cot_lp,
    cot_kl,
    rows,
    rows_turned,
    feature_result,
    tokens_result,
    weight,
    part,
    send1,
    recv1,
    send2,
    recv2,
    logits,
    grads,
    peaks,
    cots,
    stats,
    tokens,
    slots,
    spreads,
    ref32,
    core_recv,
    zsend,
    zrecv,
    in_sem,
    w_sem,
    rs_send,
    rs_recv,
    ag_send,
    ag_recv,
    st_send,
    st_recv,
    tk_send,
    tk_recv,
    core_send_sem,
    core_recv_sem,
    z_send,
    z_recv,
    out_sem,
    end_sem,
):
    width = weight.shape[2]
    rows_all = hidden.shape[0]
    count = owner_row.shape[1]
    chips = SIDE * SIDE
    rows_dev = count // chips
    levels = vocab_count // 2
    dp = lax.axis_index("dp")
    vocab = lax.axis_index("vocab")
    here = (dp // SIDE, dp % SIDE)
    level, core = vocab // 2, vocab % 2

    def along(axis, offset):
        return lax.rem(here[axis] + offset + SIDE, SIDE)

    def device(axis, offset):
        moved = along(axis, offset)
        return (moved * SIDE + here[1], vocab) if axis == 0 else (here[0] * SIDE + moved, vocab)

    def place(f, first, second):
        return (first, second) if FLOWS[f][0] == 0 else (second, first)

    barrier = pltpu.get_barrier_semaphore()
    for axis in range(2):
        for step in range(1, SIDE):
            pl.semaphore_signal(barrier, inc=1, device_id=device(axis, step), device_id_type=MESH)
    for step in range(1, vocab_count):
        pl.semaphore_signal(
            barrier, inc=1, device_id=(dp, (vocab + step) % vocab_count), device_id_type=MESH
        )
    greeted = 2 * (SIDE - 1) + vocab_count - 1

    inputs = [
        pltpu.make_async_copy(source, landing, in_sem.at[k])
        for k, (source, landing) in enumerate(
            (
                (owner_hbm, owner_row),
                (hidden_hbm, hidden),
                (cot_lp_hbm, cot_lp),
                (cot_kl_hbm, cot_kl),
                (target_hbm, target_row),
                (ref_hbm, ref),
            )
        )
    ]
    for copy in inputs:
        copy.start()

    def weight_copy(f):
        cols = pl.ds(f * width, width)
        return pltpu.make_async_copy(weight_hbm.at[:, cols], weight.at[f], w_sem.at[f])

    for f in ORDER:
        weight_copy(f).start()

    def iota(shape, dim):
        return lax.broadcasted_iota(I32, shape, dim)

    inputs[0].wait()
    rows_i, cols_i = iota((count, count), 0), iota((count, count), 1)
    diagonal = rows_i == cols_i

    def turned(row):
        return jnp.sum(jnp.where(diagonal, row, 0), axis=1, keepdims=True)

    owner_col = turned(owner_row[...].astype(F32)).astype(I32)
    alike = (owner_col == owner_row[...]) & (rows_i // rows_dev == cols_i // rows_dev)
    before_col = jnp.sum(jnp.where(alike & (cols_i < rows_i), 1.0, 0.0), axis=1, keepdims=True)
    before_row = jnp.sum(jnp.where(alike & (rows_i < cols_i), 1.0, 0.0), axis=0, keepdims=True)
    slot_count = rows_all // chips
    capacity = slot_count // chips
    slot_col = (
        owner_col * slot_count
        + (iota((count, 1), 0) // rows_dev) * capacity
        + before_col.astype(I32)
    )
    slot_row = (
        owner_row[...] * slot_count
        + (iota((1, count), 1) // rows_dev) * capacity
        + before_row.astype(I32)
    )
    placing = slot_col == iota((count, rows_all), 1)
    inputs[1].wait()
    rows[...] = jnp.dot(
        jnp.where(placing, 1.0, 0.0).astype(BF16), hidden[...], preferred_element_type=F32
    ).astype(BF16)

    def rs_copy(s, f, kind):
        axis, way = FLOWS[f]
        stage, role = kind // 3, kind % 3
        if stage == 1:
            axis = 1 - axis
        source, landing = (send1, recv1) if stage == 0 else (send2, recv2)
        return pltpu.make_async_remote_copy(
            src_ref=source.at[s, f, role],
            dst_ref=landing.at[s, f, role],
            send_sem=rs_send.at[s, stage],
            recv_sem=rs_recv.at[s, kind, f],
            device_id=device(axis, 2 if kind == 3 else -way if role == 1 else way),
            device_id_type=MESH,
        )

    def first_blocks(s, f, offset):
        first = along(FLOWS[f][0], offset)
        return [part[(s, f) + place(f, first, k)] for k in range(SIDE)]

    def second_block(s, f, offset):
        axis = FLOWS[f][0]
        return part[(s, f) + place(f, here[axis], along(1 - axis, offset))]

    def multiply(f):
        weight_copy(f).wait()
        product = jnp.dot(rows[...], weight[f], preferred_element_type=F32)
        product = product.reshape(SIDE, SIDE, rows_dev, width)
        part[0, f] = product[:, :, 0:ROWS]
        part[1, f] = product[:, :, ROWS:rows_dev]

    def first_ahead(s, f):
        encode(first_blocks(s, f, 2), send1.at[s, f, 0])
        rs_copy(s, f, 0).start()

    def first_back(s, f):
        encode(first_blocks(s, f, -FLOWS[f][1]), send1.at[s, f, 1])
        rs_copy(s, f, 1).start()

    def first_relay(s):
        for f in ORDER:
            rs_copy(s, f, 0).wait_recv()
            own = first_blocks(s, f, FLOWS[f][1])
            arrived = recv1.at[s, f, 0]
            encode(
                [own[k] + decode(arrived, k, width) for k in range(SIDE)], send1.at[s, f, 2]
            )
            rs_copy(s, f, 2).start()

    def first_sum(s):
        for f in ORDER:
            rs_copy(s, f, 1).wait_recv()
            rs_copy(s, f, 2).wait_recv()
            axis, way = FLOWS[f]
            for k in range(SIDE):
                spot = (s, f) + place(f, here[axis], k)
                part[spot] = (
                    part[spot]
                    + decode(recv1.at[s, f, 1], k, width)
                    + decode(recv1.at[s, f, 2], k, width)
                )
            for role, offset in ((0, 2), (1, -way), (2, way)):
                encode([second_block(s, f, offset)], send2.at[s, f, role])
                rs_copy(s, f, 3 + role).start()

    def second_sum(s):
        peak = jnp.full((ROWS, LANES), -jnp.inf, F32)
        for f in ORDER:
            for kind in (3, 4, 5):
                rs_copy(s, f, kind).wait_recv()
            done = (
                second_block(s, f, 0)
                + decode(recv2.at[s, f, 0], 0, width)
                + decode(recv2.at[s, f, 1], 0, width)
                + decode(recv2.at[s, f, 2], 0, width)
            )
            logits[s, f] = done
            for t in range(width // LANES):
                peak = jnp.maximum(peak, done[:, t * LANES : (t + 1) * LANES])
        peaks[s] = peak

    def ref_piece(s, f):
        return ref32[s * ROWS : (s + 1) * ROWS, f * width : (f + 1) * width]

    def lane_sum(values):
        total = values[:, 0:LANES]
        for t in range(1, width // LANES):
            total = total + values[:, t * LANES : (t + 1) * LANES]
        return total

    first_col = vocab * (4 * width)
    lane = iota((ROWS, LANES), 1)

    def my_cots(s):
        start = pl.multiple_of(dp * rows_dev, rows_dev) + s * ROWS
        mine = cots[pl.ds(pl.multiple_of(start, ROWS), ROWS), :]
        return mine[:, 0:1], mine[:, 1:2], mine[:, 2:3].astype(I32)

    def hit(f, target):
        return first_col + f * width + iota((ROWS, width), 1) == target

    def ref_stats(s):
        peak = jnp.full((ROWS, 1), -jnp.inf, F32)
        for f in range(4):
            peak = jnp.maximum(peak, jnp.max(ref_piece(s, f), axis=1, keepdims=True))
        mass = jnp.zeros((ROWS, LANES), F32)
        for f in range(4):
            mass = mass + lane_sum(jnp.exp(ref_piece(s, f) - peak))
        return peak, jnp.sum(mass, axis=1, keepdims=True)

    def stats_copy(s, step):
        return pltpu.make_async_remote_copy(
            src_ref=stats.at[s, vocab],
            dst_ref=stats.at[s, vocab],
            send_sem=st_send.at[s],
            recv_sem=st_recv.at[s],
            device_id=(dp, (vocab + step) % vocab_count),
            device_id_type=MESH,
        )

    def stats_send(s, ref_side):
        target = my_cots(s)[2]
        peak = jnp.max(peaks[s], axis=1, keepdims=True)
        mass = cross = picked = jnp.zeros((ROWS, LANES), F32)
        for f in range(4):
            values = logits[s, f]
            weights = jnp.exp(values - peak)
            mass = mass + lane_sum(weights)
            cross = cross + lane_sum(weights * (values - ref_piece(s, f)))
            picked = picked + lane_sum(jnp.where(hit(f, target), values, 0.0))
        mass, cross, picked = [
            jnp.sum(value, axis=1, keepdims=True) for value in (mass, cross, picked)
        ]
        packed = jnp.zeros((ROWS, LANES), F32)
        for k, value in enumerate((peak, mass, cross) + ref_side + (picked,)):
            packed = packed + jnp.where(lane == k, value, 0.0)
        stats[s, vocab] = packed
        for step in range(1, vocab_count):
            stats_copy(s, step).start()

    def other_stats(s):
        return stats.at[s, pl.ds(0, vocab_count - 1)]

    def stats_finish(s):
        pltpu.make_async_copy(other_stats(s), other_stats(s), st_recv.at[s]).wait()
        every = [stats[s, k] for k in range(vocab_count)]
        peak, ref_peak = every[0][:, 0:1], every[0][:, 3:4]
        for tile in every[1:]:
            peak = jnp.maximum(peak, tile[:, 0:1])
            ref_peak = jnp.maximum(ref_peak, tile[:, 3:4])
        mass, cross, ref_mass, picked = 0.0, 0.0, 0.0, 0.0
        for tile in every:
            scale = jnp.exp(tile[:, 0:1] - peak)
            mass = mass + tile[:, 1:2] * scale
            cross = cross + tile[:, 2:3] * scale
            ref_mass = ref_mass + tile[:, 4:5] * jnp.exp(tile[:, 3:4] - ref_peak)
            picked = picked + tile[:, 5:6]
        norm = peak + jnp.log(mass)
        ref_norm = ref_peak + jnp.log(ref_mass)
        row_kl = cross / mass - norm + ref_norm
        tokens[here[0], here[1], s * ROWS : (s + 1) * ROWS] = (
            jnp.where(lane == 0, picked - norm, 0.0)
            + jnp.where(lane == 1, row_kl, 0.0)
            + jnp.where(lane == 2, norm, 0.0)
        )
        return norm, ref_norm - norm - row_kl

    half = width // 2

    def gradients(s, norm, shift):
        lp, kl, target = my_cots(s)
        for f in ORDER:
            values = logits[s, f]
            probs = jnp.exp(values - norm)
            excess = values - ref_piece(s, f) + shift
            result = jnp.where(hit(f, target), lp, 0.0) + probs * (kl * excess - lp)
            result = jnp.concatenate([result[:, 0:half], result[:, half:width]], axis=0)
            grads[s, f, here[0], here[1]] = result.astype(BF16)
            for kind in (0, 1, 2):
                ag_copy(s, f, kind).start()
            line_go(s, f, 0)

    def relay_copy(buffer, f, kind, straight, send_sem, recv_sem):
        axis, way = FLOWS[f]
        other = 1 - axis
        if kind < 3:
            relayed = kind == 2 and not straight
            spot = place(f, along(axis, -way if relayed else 0), here[other])
            to = device(axis, 2 if kind == 2 and straight else -way if kind == 1 else way)
        else:
            spot = place(f, slice(None), along(other, -way if kind == 5 else 0))
            to = device(other, -way if kind == 4 else way)
        block = buffer.at[spot]
        return pltpu.make_async_remote_copy(
            src_ref=block,
            dst_ref=block,
            send_sem=send_sem,
            recv_sem=recv_sem,
            device_id=to,
            device_id_type=MESH,
        )

    def ag_copy(g, f, kind):
        return relay_copy(
            grads.at[g, f], f, kind, True, ag_send.at[g, kind // 3], ag_recv.at[g, kind, f]
        )

    def line_go(g, f, offset):
        axis, way = FLOWS[f]
        block = grads.at[(g, f) + place(f, along(axis, offset), here[1 - axis])]
        for kind, to in ((3, way), (4, -way)):
            pltpu.make_async_remote_copy(
                src_ref=block,
                dst_ref=block,
                send_sem=ag_send.at[g, 1],
                recv_sem=ag_recv.at[g, kind, f],
                device_id=device(1 - axis, to),
                device_id_type=MESH,
            ).start()

    def line_pass(g):
        for kind in (0, 1, 2):
            for f in ORDER:
                ag_copy(g, f, kind).wait_recv()
                line_go(g, f, (-FLOWS[f][1], FLOWS[f][1], 2)[kind])

    def ag_pass(g, waits, kinds):
        for f in ORDER:
            for kind in waits:
                ag_copy(g, f, kind).wait_recv()
            for kind in kinds:
                ag_copy(g, f, kind).start()

    def tokens_copy(axis, step):
        block = tokens.at[here] if axis == 1 else tokens.at[here[0]]
        return pltpu.make_async_remote_copy(
            src_ref=block,
            dst_ref=block,
            send_sem=tk_send.at[axis],
            recv_sem=tk_recv.at[axis],
            device_id=device(axis, step),
            device_id_type=MESH,
        )

    def tokens_go(axis):
        for step in range(1, SIDE):
            tokens_copy(axis, step).start()

    def tokens_moved(axis, sem):
        moved = tokens.at[0, pl.ds(0, 3)] if axis == 1 else tokens.at[pl.ds(0, 3)]
        pltpu.make_async_copy(moved, moved, sem.at[axis]).wait()

    def out_copy(g, f):
        return pltpu.make_async_copy(grads.at[g, f], grads_out.at[g, f], out_sem.at[g, f])

    def group_token(g, shape, dim):
        order = iota(shape, dim)
        return (order // ROWS) * rows_dev + g * ROWS + lax.rem(order, ROWS)

    members = count // GROUPS

    def spread(g):
        shape = (count, members)
        chosen = iota(shape, 0) == group_token(g, shape, 1)
        slot_of = jnp.sum(jnp.where(chosen, slot_col.astype(F32), 0.0), axis=0, keepdims=True)
        matches = iota((rows_all, members), 0) == slot_of.astype(I32)
        return jnp.where(matches, 1.0, 0.0).astype(BF16)

    def feature_step(g):
        total = jnp.zeros((members, rows.shape[1]), F32)
        for f in ORDER:
            ag_copy(g, f, 4).wait_recv()
            ag_copy(g, f, 5).wait_recv()
            out_copy(g, f).start()
            for h in range(2):
                piece = grads[g, f, :, :, h * ROWS : (h + 1) * ROWS, :].reshape(members, half)
                total = total + lax.dot_general(
                    piece,
                    weight[f, :, h * half : (h + 1) * half],
                    (((1,), (1,)), ((), ())),
                    preferred_element_type=F32,
                )
        high = total.astype(BF16)
        rest = total - high.astype(F32)
        middle = rest.astype(BF16)
        low = (rest - middle.astype(F32)).astype(BF16)
        return high, middle, low

    def placed(g, l, split):
        total = 0.0
        for piece in split:
            total = total + jnp.dot(spreads[g, l], piece, preferred_element_type=F32)
        return total.reshape(slots.shape[1:])

    for f in ORDER:
        multiply(f)
        if f == 0:
            pl.semaphore_wait(barrier, greeted)
        first_ahead(0, f)
        first_back(0, f)
    first_relay(0)
    for f in ORDER:
        first_ahead(1, f)
    for copy in inputs[2:]:
        copy.wait()
    ref32[...] = ref[...].astype(F32)
    lp_col = jnp.sum(jnp.where(placing, cot_lp[...], 0.0), axis=1, keepdims=True)
    kl_col = jnp.sum(jnp.where(placing, cot_kl[...], 0.0), axis=1, keepdims=True)
    target_col = turned(target_row[...].astype(F32))
    lane_all = iota((count, LANES), 1)
    cots[...] = (
        jnp.where(lane_all == 0, lp_col, 0.0)
        + jnp.where(lane_all == 1, kl_col, 0.0)
        + jnp.where(lane_all == 2, target_col, 0.0)
    )
    first_sum(0)
    for f in ORDER:
        first_back(1, f)
    ref_side = [ref_stats(0), ref_stats(1)]
    first_relay(1)
    second_sum(0)
    stats_send(0, ref_side[0])
    first_sum(1)
    gradients(0, *stats_finish(0))
    second_sum(1)
    stats_send(1, ref_side[1])
    line_pass(0)
    gradients(1, *stats_finish(1))
    ag_pass(0, (3,), (5,))
    line_pass(1)
    tokens_go(1)
    for g in range(GROUPS):
        to_slots = spread(g)
        spreads[g] = to_slots.reshape(spreads.shape[1:])
        rows_turned[:, g * members : (g + 1) * members] = lax.dot_general(
            hidden[...], to_slots, (((0,), (0,)), ((), ())), preferred_element_type=F32
        ).astype(BF16)
    rows_copy = pltpu.make_async_copy(rows_turned, rows_out, end_sem.at[0])
    rows_copy.start()
    ag_pass(1, (3,), (5,))
    tokens_moved(1, tk_recv)
    tokens_go(0)
    split = feature_step(0)
    for l in range(levels):
        slots[l] = placed(0, l, split)

    def core_copy(l):
        return pltpu.make_async_remote_copy(
            src_ref=slots.at[l, 1 - core],
            dst_ref=core_recv.at[l],
            send_sem=core_send_sem.at[l],
            recv_sem=core_recv_sem.at[l],
            device_id=(dp, level * 2 + 1 - core),
            device_id_type=MESH,
        )

    turns = [step for step in (2, 1, 3, 0) if step < levels]
    split = feature_step(1)
    for step in turns:
        l = lax.rem(level + step, levels)
        slots[l] = slots[l] + placed(1, l, split)
        core_copy(l).start()

    slot_rows = slots.shape[2]
    feature_width = slots.shape[3]

    def pair_sum(l):
        core_copy(l).wait_recv()
        return slots[l, core] + core_recv[l]

    def z_copy(step):
        return pltpu.make_async_remote_copy(
            src_ref=zsend.at[step],
            dst_ref=zrecv.at[step],
            send_sem=z_send.at[step],
            recv_sem=z_recv.at[step],
            device_id=(dp, ((level + step) % levels) * 2 + core),
            device_id_type=MESH,
        )

    for step in turns:
        if step > 0:
            both = pair_sum(lax.rem(level + step, levels))
            encode([both[k : k + ROWS] for k in range(0, slot_rows, ROWS)], zsend.at[step])
            z_copy(step).start()
    tokens_moved(0, tk_recv)
    everyone = tokens[...].reshape(count, LANES)
    mine_slots = slot_col == dp * slot_count + lane_all
    mine_slots = mine_slots & (lane_all < slot_count)
    for k in range(3):
        tokens_result[k : k + 1, :] = jnp.sum(
            jnp.where(mine_slots, everyone[:, k : k + 1], 0.0), axis=0, keepdims=True
        )

    tokens_copied = pltpu.make_async_copy(tokens_result, tokens_out, end_sem.at[1])
    tokens_copied.start()
    total = pair_sum(level)
    for step in range(1, levels):
        z_copy(step).wait_recv()
    pieces_out = []
    for k in range(slot_rows // ROWS):
        block = total[k * ROWS : (k + 1) * ROWS]
        for step in range(1, levels):
            block = block + decode(zrecv.at[step], k, feature_width)
        pieces_out.append(block)
    feature_result[...] = jnp.concatenate(pieces_out, axis=0).astype(BF16)
    feature_copied = pltpu.make_async_copy(feature_result, feature_out, end_sem.at[2])
    feature_copied.start()

    def left(source, sem):
        pltpu.make_async_copy(source, source, sem).wait()

    for s in range(GROUPS):
        left(send1.at[s], rs_send.at[s, 0])
        left(send2.at[s], rs_send.at[s, 1])
    for g in range(GROUPS):
        left(grads.at[g, :, 0, pl.ds(0, 3)], ag_send.at[g, 0])
        left(grads.at[g, pl.ds(0, 3)], ag_send.at[g, 1])
        for f in range(4):
            out_copy(g, f).wait()
        left(other_stats(g), st_send.at[g])
    for axis in range(2):
        tokens_moved(axis, tk_send)
    for l in range(levels):
        core_copy(l).wait_send()
    for step in range(1, levels):
        z_copy(step).wait_send()
    rows_copy.wait()
    tokens_copied.wait()
    feature_copied.wait()


def weight_kernel(
    rows_in,
    grads_in,
    feature_in,
    tokens_in,
    out,
    feature_out,
    first,
    second,
    third,
    rows,
    grads,
    tokens,
    small,
    result,
    in_sem,
    out_sem,
):
    width = grads.shape[5]
    members = rows.shape[1] // GROUPS

    def load(f):
        return pltpu.make_async_copy(grads_in.at[:, f], grads.at[f], in_sem.at[f])

    def store(f, h):
        cols = pl.ds((2 * f + h) * width, width)
        return pltpu.make_async_copy(result.at[f, h], out.at[:, cols], out_sem.at[f, h])

    rows_copy = pltpu.make_async_copy(rows_in, rows, in_sem.at[4])
    rows_copy.start()
    for f in range(4):
        load(f).start()
    tokens_copy = pltpu.make_async_copy(tokens_in, tokens, in_sem.at[5])
    tokens_copy.start()
    feature_copy = pltpu.make_async_copy(feature_in, feature_out, in_sem.at[6])
    feature_copy.start()
    rows_copy.wait()
    for f in range(4):
        load(f).wait()
        for h in range(2):
            block = jnp.concatenate(
                [
                    grads[f, g, :, :, h * ROWS : (h + 1) * ROWS, :].reshape(members, width)
                    for g in range(GROUPS)
                ],
                axis=0,
            )
            result[f, h] = jnp.dot(rows[...], block, preferred_element_type=F32).astype(BF16)
            store(f, h).start()
    tokens_copy.wait()
    outs = []
    for k, token_out in enumerate((first, second, third)):
        small[k] = tokens[k : k + 1, 0 : small.shape[2]]
        outs.append(pltpu.make_async_copy(small.at[k], token_out, in_sem.at[7 + k]))
        outs[-1].start()
    feature_copy.wait()
    for copy in outs:
        copy.wait()
    for f in range(4):
        for h in range(2):
            store(f, h).wait()


def per_device(
    vocab_count, pol_hidden, pol_weight, ref_logits, targets, owners, grad_logprob, grad_kl
):
    all_slots, depth = pol_hidden.shape
    cols = pol_weight.shape[1]
    rows_dev = ref_logits.shape[0]
    count = owners.shape[0]
    chips = SIDE * SIDE
    width = cols // 4
    slot_count = all_slots // chips
    levels = vocab_count // 2
    slot_rows = all_slots // vocab_count
    unit1 = (GROUPS, 4, 3, ROWS, SIDE * width // 2 + LANES)
    unit2 = (GROUPS, 4, 3, ROWS, width // 2 + LANES)
    unit3 = (levels, ROWS, slot_rows // ROWS * depth // 2 + LANES)
    grads_shape = (GROUPS, 4, SIDE, SIDE, rows_dev, width // 2)
    anywhere = pl.BlockSpec(memory_space=pl.ANY)
    flops = 2 * count * depth * cols * 2
    grads, rows, feature, tokens = pl.pallas_call(
        functools.partial(head_kernel, vocab_count),
        out_shape=(
            jax.ShapeDtypeStruct(grads_shape, BF16),
            jax.ShapeDtypeStruct((depth, count), BF16),
            jax.ShapeDtypeStruct((slot_rows, depth), BF16),
            jax.ShapeDtypeStruct((8, LANES), F32),
        ),
        in_specs=[pl.BlockSpec(memory_space=pltpu.HBM)] * 7,
        out_specs=(anywhere,) * 4,
        scratch_shapes=[
            pltpu.VMEM((all_slots, depth), BF16),
            pltpu.VMEM((rows_dev, cols), BF16),
            pltpu.VMEM((1, count), I32),
            pltpu.VMEM((1, count), I32),
            pltpu.VMEM((1, all_slots), F32),
            pltpu.VMEM((1, all_slots), F32),
            pltpu.VMEM((count, depth), BF16),
            pltpu.VMEM((depth, count), BF16),
            pltpu.VMEM((slot_rows, depth), BF16),
            pltpu.VMEM((8, LANES), F32),
            pltpu.VMEM((4, depth, width), BF16),
            pltpu.VMEM((GROUPS, 4, SIDE, SIDE, ROWS, width), F32),
            pltpu.VMEM(unit1, I32),
            pltpu.VMEM(unit1, I32),
            pltpu.VMEM(unit2, I32),
            pltpu.VMEM(unit2, I32),
            pltpu.VMEM((GROUPS, 4, ROWS, width), F32),
            pltpu.VMEM(grads_shape, BF16),
            pltpu.VMEM((GROUPS, ROWS, LANES), F32),
            pltpu.VMEM((count, LANES), F32),
            pltpu.VMEM((GROUPS, vocab_count, ROWS, LANES), F32),
            pltpu.VMEM((SIDE, SIDE, rows_dev, LANES), F32),
            pltpu.VMEM((levels, 2, slot_rows, depth), F32),
            pltpu.VMEM((GROUPS, levels, all_slots // levels, count // GROUPS), BF16),
            pltpu.VMEM((rows_dev, cols), F32),
            pltpu.VMEM((levels, slot_rows, depth), F32),
            pltpu.VMEM(unit3, I32),
            pltpu.VMEM(unit3, I32),
            pltpu.SemaphoreType.DMA((6,)),
            pltpu.SemaphoreType.DMA((4,)),
            pltpu.SemaphoreType.DMA((GROUPS, 2)),
            pltpu.SemaphoreType.DMA((GROUPS, 6, 4)),
            pltpu.SemaphoreType.DMA((GROUPS, 2)),
            pltpu.SemaphoreType.DMA((GROUPS, 6, 4)),
            pltpu.SemaphoreType.DMA((GROUPS,)),
            pltpu.SemaphoreType.DMA((GROUPS,)),
            pltpu.SemaphoreType.DMA((2,)),
            pltpu.SemaphoreType.DMA((2,)),
            pltpu.SemaphoreType.DMA((levels,)),
            pltpu.SemaphoreType.DMA((levels,)),
            pltpu.SemaphoreType.DMA((levels,)),
            pltpu.SemaphoreType.DMA((levels,)),
            pltpu.SemaphoreType.DMA((GROUPS, 4)),
            pltpu.SemaphoreType.DMA((3,)),
        ],
        compiler_params=pltpu.CompilerParams(
            collective_id=0, has_side_effects=True, vmem_limit_bytes=60 * 2**20
        ),
        cost_estimate=pl.CostEstimate(
            flops=flops, bytes_accessed=3 * depth * cols, transcendentals=3 * rows_dev * cols
        ),
        name="head",
    )(
        pol_hidden,
        pol_weight,
        ref_logits,
        targets.reshape(1, count),
        owners.reshape(1, count),
        grad_logprob.reshape(1, all_slots),
        grad_kl.reshape(1, all_slots),
    )
    token_shape = jax.ShapeDtypeStruct((1, slot_count), F32)
    weight_grad, feature, first, second, third = pl.pallas_call(
        weight_kernel,
        out_shape=(
            jax.ShapeDtypeStruct((depth, cols), BF16),
            jax.ShapeDtypeStruct((slot_rows, depth), BF16),
            token_shape,
            token_shape,
            token_shape,
        ),
        in_specs=[anywhere] * 4,
        out_specs=(anywhere,) * 5,
        scratch_shapes=[
            pltpu.VMEM((depth, count), BF16),
            pltpu.VMEM((4, GROUPS) + grads_shape[2:], BF16),
            pltpu.VMEM((8, LANES), F32),
            pltpu.VMEM((3, 1, slot_count), F32),
            pltpu.VMEM((4, 2, depth, width // 2), BF16),
            pltpu.SemaphoreType.DMA((10,)),
            pltpu.SemaphoreType.DMA((4, 2)),
        ],
        compiler_params=pltpu.CompilerParams(vmem_limit_bytes=60 * 2**20),
        cost_estimate=pl.CostEstimate(
            flops=2 * count * depth * cols,
            bytes_accessed=2 * (depth + count) * cols,
            transcendentals=0,
        ),
        name="weight_grad",
    )(rows, grads, feature, tokens)
    return (
        first.reshape(slot_count),
        second.reshape(slot_count),
        third.reshape(slot_count),
        feature,
        weight_grad,
    )


def solution(mesh):
    in_specs = (P(None, "dp"), P("dp", "vocab"), P("dp", "vocab"), P(), P(), P(), P())
    out_specs = (P("dp"), P("dp"), P("dp"), P("vocab", "dp"), P("dp", "vocab"))
    return jax.shard_map(
        functools.partial(per_device, mesh.shape["vocab"]),
        mesh=mesh,
        in_specs=in_specs,
        out_specs=out_specs,
        check_vma=False,
    )
```
